32 devices in a mesh: seq: 4 (over x, core), tensor: 8 (over z, y).
Axes of the slice: x: 2, y: 2, z: 4, core: 2. Of those that a mesh axis runs over, the one named last changes fastest.
Arguments:
- tokens: bfloat16 [256, 2048], P(('seq', 'tensor')), may hold values from -6 to 6
- attn_gain: bfloat16 [2048], replicated, may hold values from 0.25 to 1.75
- w_qkv: bfloat16 [2048, 3, 2048], P(None, None, 'tensor'), may hold values from -0.125 to 0.125
- q_gain: bfloat16 [2048], P('tensor'), may hold values from 0.25 to 1.75
- k_gain: bfloat16 [2048], P('tensor'), may hold values from 0.25 to 1.75
- w_out: bfloat16 [2048, 2048], P('tensor'), may hold values from -0.125 to 0.125
- prefix_keys: bfloat16 [4, 2048, 2048], P('seq', None, 'tensor'), may hold values from -150 to 150
- prefix_values: bfloat16 [4, 2048, 2048], P('seq', None, 'tensor'), may hold values from -6 to 6
- segments: int32 [256], replicated, may hold values from 0 to 15, never falling along the last dimension, each value on 1 to 64 neighbouring positions
- request_group: int32 [16], replicated, may hold values from 0 to 1
- prefix_owner: int32 [2], replicated, may hold values from 0 to 3, as said below
- mlp_gain: bfloat16 [2048], replicated, may hold values from 0.25 to 1.75
- expert_ids: int32 [256, 8], P(('seq', 'tensor')), may hold values from 0 to 15, all different within a row; in each aligned block of 8 rows (0 to 7, 8 to 15, ...) at most 8 rows name the same one
- gate_weights: float32 [256, 8], P(('seq', 'tensor')), may hold values from 0.05 to 0.5
- w_gate: bfloat16 [32, 2048, 512], P(('tensor', 'seq')), may hold values from -0.125 to 0.125
- w_up: bfloat16 [32, 2048, 512], P(('tensor', 'seq')), may hold values from -0.125 to 0.125
- w_down: bfloat16 [32, 512, 2048], P(('tensor', 'seq')), may hold values from -0.1875 to 0.1875
Outputs:
- output: bfloat16 [256, 2048], P(('seq', 'tensor'))
- new_keys: bfloat16 [256, 2048], P('seq', 'tensor')
- new_values: bfloat16 [256, 2048], P('seq', 'tensor')
The draws below stay inside these ranges and needn't reach their ends.
Inputs may be any that keep to these rules, and one draw needn't show every extreme that they name: `segments`: each request's tokens are consecutive; a request has at most 64 tokens, and some request has exactly 64. `prefix_owner`: distinct slots. `expert_ids`: a token's experts are distinct; among the 8 rows of one device no expert is named more than 8 times, and that count is reached.
All inputs are finite; a program needn't handle non-finite values.
Results may differ from the reference program's by a relative error of at most 0.017.
Values may be sent and summed in bfloat16 or wider, within the bound.
A program may use at most 64 MiB of HBM per device.

```python
import math
import jax
import jax.numpy as jnp
import numpy as np
from jax import lax

D = 2048
HEADS = 16
HD = 128
FF = 1024
TOP = 8
TOK_DEV = 8
PREFIX = 2048
EXPERTS = 16
UNITS = 512
TOK = 64
TOKENS = 256
GROUPS = 2
REQS = 16
CAP = 8
N_SEQ = 4


def draw_prefix_keys(key, part):
    base = jax.random.normal(key, (N_SEQ, PREFIX, D), jnp.float32)
    return jnp.clip(base, -150.0, 150.0).astype(jnp.bfloat16)


def draw_prefix_owner(key, part):
    others = jax.random.permutation(jax.random.fold_in(key, 11), N_SEQ - 1)[:GROUPS - 1].astype(jnp.int32)
    chosen = jnp.concatenate([others, jnp.full((1,), N_SEQ - 1, jnp.int32)], axis=0)
    order = jax.random.permutation(jax.random.fold_in(key, 13), GROUPS)
    return chosen[order].astype(jnp.int32)


def plant(drawn, stream_key, smallest, high):
    place = [jax.random.randint(jax.random.fold_in(stream_key, axis), (), 0, length) for axis, length in enumerate(drawn.shape)]
    widest = drawn.shape.index(max(drawn.shape))
    next_to = place[:widest] + [(place[widest] + 1) % drawn.shape[widest]] + place[widest + 1:]
    return drawn.at[tuple(place)].set(smallest).at[tuple(next_to)].set(high)


def levels(rng, extent, cuts, least, top_value):
    def one(dim, blocks):
        steps = jax.random.uniform(jax.random.fold_in(jax.random.fold_in(rng, 6), dim), (blocks,), jnp.float32, least / len(cuts), top_value / len(cuts))
        return jnp.repeat(jnp.exp(steps), extent[dim] // blocks).reshape((-1,) + (1,) * (len(extent) - dim - 1))

    factor_of = one(*cuts[0])
    for cut in cuts[1:]:
        factor_of = factor_of * one(*cut)
    return factor_of


def split_up(number_of, total, bound, lean):
    weights = [(1 << 20) // math.isqrt(grade ** lean) + 1 for grade in range(2, number_of + 1)]
    rest, given = total - bound - (number_of - 1), [1] * (number_of - 1)
    while rest > 0:
        free = [i for i in range(number_of - 1) if given[i] < bound]
        mass, budget = sum([weights[i] for i in free]), rest
        for i in free:
            extra = min(bound - given[i], max(1, budget * weights[i] // mass), rest)
            given[i] = given[i] + extra
            rest = rest - extra
    return np.array([bound] + given)


def uneven(rng, count, total, most, lean):
    if count == 2:
        one = jax.random.randint(rng, (), max(1, total - most), min(most, total - 1) + 1)
        return jnp.stack([one, total - one])
    sizes = jnp.asarray(split_up(count, total, most, lean), jnp.int32)
    couples = (count - 1) // 2
    donor, taker = sizes[1:1 + 2 * couples:2], sizes[2:2 + 2 * couples:2]
    slack = jnp.minimum(donor - 1, most - taker)
    moved = jax.random.randint(jax.random.fold_in(rng, 1), (couples,), 0, 1 << 20) % (slack + 1)
    sizes = sizes.at[1:1 + 2 * couples:2].set(donor - moved).at[2:2 + 2 * couples:2].set(taker + moved)
    return sizes[jax.random.permutation(jax.random.fold_in(rng, 2), count)]


def assign_block(own_key, own, number, rows, number_of, top, limit, slope):
    sequence = jax.random.permutation(own_key, number_of)
    crowded, ordinary = portions_of(number_of, rows * top, limit, slope, True), portions_of(number_of, rows * top, limit, slope, False)
    places = jnp.arange(number_of)

    def named(sizes, turn):
        used = int((sizes > 0).sum())
        fixed = max(1, used // 4)
        shifted = fixed + (places - fixed + turn * (used - fixed)) % max(1, number_of - fixed)
        return jnp.zeros((number_of,), jnp.int32).at[sequence[jnp.where(places < fixed, places, shifted)]].set(jnp.asarray(sizes, jnp.int32))

    sizes = jnp.where(number % 4 == 0, named(crowded, number // 4), named(ordinary, number - number // 4 - 1))
    mixed = jax.random.permutation(jax.random.fold_in(own, 3), number_of)
    source_of, taker = mixed[0:number_of // 2 * 2:2], mixed[1:number_of // 2 * 2:2]
    room = jnp.minimum(sizes[source_of] - 1, limit - sizes[taker]) // 2
    room = jnp.where((source_of == sequence[0]) | (taker == sequence[0]) | (sizes[taker] == 0), 0, jnp.maximum(room, 0))
    shifted = jax.random.randint(jax.random.fold_in(own, 4), (number_of // 2,), 0, 1 << 20) % (room + 1)
    sizes = sizes.at[source_of].add(-shifted).at[taker].add(shifted)
    items = jnp.searchsorted(jnp.cumsum(sizes), jnp.arange(rows * top), side="right").astype(jnp.int32)
    table = items.reshape(top, rows).T
    table = table[jax.random.permutation(jax.random.fold_in(own, 1), rows)]
    turn = jax.random.randint(jax.random.fold_in(own, 2), (rows, 1), 0, top)
    return jnp.take_along_axis(table, (jnp.arange(top)[None, :] + turn) % top, axis=1)


def portions_of(number_of, total, reach, lean, full):
    portions = [(1 << 20) // math.isqrt(standing ** lean) + 1 for standing in range(1, number_of + 1)]
    largest = reach if full else min(reach, max(-(-total // number_of), total * portions[0] // sum(portions)))
    least = 1 if total - largest >= number_of - 1 else 0
    holding, rest = [largest] + [least] * (number_of - 1), total - largest - least * (number_of - 1)
    while rest > 0:
        candidates = [i for i in range(1, number_of) if holding[i] < largest] or [i for i in range(1, number_of) if holding[i] < reach]
        mass, remaining = sum([portions[i] for i in candidates]), rest
        for i in candidates:
            addition = min(reach - holding[i], max(1, remaining * portions[i] // mass), rest)
            holding[i] = holding[i] + addition
            rest = rest - addition
    return np.array(holding)


def normal_values(stream_key, extent, deviation, bound, shards=(), kind=jnp.bfloat16):
    values = jax.random.normal(stream_key, extent, jnp.float32) * deviation
    if len(shards) > 0:
        values = levels(stream_key, extent, shards, -0.22, 0.18) * values
    return jnp.clip(values, min=-bound, max=bound).astype(kind)


def setup_inputs(seed: int = 0) -> dict:
    streams_of = jax.random.split(jax.random.key(seed), 18)
    tokens = normal_values(streams_of[0], (TOKENS, D), 1.0, 6.0, ((0, 32),))
    attn_gain = jnp.clip(1.0 + 0.15 * jax.random.normal(streams_of[1], (D,), jnp.float32), 0.25, 1.75).astype(jnp.bfloat16)
    w_qkv = normal_values(streams_of[2], (D, 3, D), D ** -0.5, 0.125, ((2, 8),))
    q_gain = jnp.clip(1.0 + 0.15 * jax.random.normal(streams_of[3], (D,), jnp.float32), 0.25, 1.75).astype(jnp.bfloat16)
    k_gain = jnp.clip(1.0 + 0.15 * jax.random.normal(streams_of[4], (D,), jnp.float32), 0.25, 1.75).astype(jnp.bfloat16)
    w_out = normal_values(streams_of[5], (D, D), D ** -0.5, 0.125, ((0, 8),))
    prefix_keys = draw_prefix_keys(jax.random.fold_in(streams_of[17], 71), 0)
    prefix_values = normal_values(streams_of[7], (N_SEQ, PREFIX, D), 1.0, 6.0, ((0, 4), (2, 8)))
    segments = jnp.searchsorted(jnp.cumsum(uneven(streams_of[8], REQS, TOKENS, TOK, 2)), jnp.arange(TOKENS), side="right").astype(jnp.int32)
    request_group = plant(jax.random.randint(streams_of[9], (REQS,), 0, GROUPS), jax.random.fold_in(streams_of[9], 1), 0, GROUPS - 1).astype(jnp.int32)
    prefix_owner = draw_prefix_owner(jax.random.fold_in(streams_of[17], 71), 0)
    mlp_gain = jnp.clip(1.0 + 0.15 * jax.random.normal(streams_of[11], (D,), jnp.float32), 0.25, 1.75).astype(jnp.bfloat16)
    expert_ids_keys = jax.random.split(jax.random.fold_in(streams_of[12], 1), TOKENS // TOK_DEV)
    expert_ids_turns = jax.random.permutation(jax.random.fold_in(streams_of[12], 3), TOKENS // TOK_DEV)
    expert_ids = jax.vmap(lambda own, number: assign_block(jax.random.fold_in(streams_of[12], 2), own, number, TOK_DEV, EXPERTS, TOP, CAP, 2))(expert_ids_keys, expert_ids_turns).reshape((TOKENS, TOP))
    gate_weights = jnp.clip(jnp.exp(math.log(0.5) - 2.3025851 * jax.random.uniform(streams_of[13], (TOKENS, TOP), jnp.float32) ** levels(streams_of[13], (TOKENS, TOP), ((0, 32),), -0.2, 0.2)), 0.05, 0.5)
    w_gate = normal_values(streams_of[14], (EXPERTS * FF // UNITS, D, UNITS), D ** -0.5, 0.125, ((0, 32),))
    w_up = normal_values(streams_of[15], (EXPERTS * FF // UNITS, D, UNITS), D ** -0.5, 0.125, ((0, 32),))
    w_down = normal_values(streams_of[16], (EXPERTS * FF // UNITS, UNITS, D), FF ** -0.5, 0.1875, ((0, 32),))
    return dict(tokens=tokens, attn_gain=attn_gain, w_qkv=w_qkv, q_gain=q_gain, k_gain=k_gain, w_out=w_out, prefix_keys=prefix_keys, prefix_values=prefix_values, segments=segments, request_group=request_group, prefix_owner=prefix_owner, mlp_gain=mlp_gain, expert_ids=expert_ids, gate_weights=gate_weights, w_gate=w_gate, w_up=w_up, w_down=w_down)


def rms_scale(values, gain):
    mean_square = lax.optimization_barrier(jnp.mean(values * values, axis=-1, keepdims=True))
    return values * lax.rsqrt(mean_square + 1e-05) * gain.astype(jnp.float32)

def reference(tokens, attn_gain, w_qkv, q_gain, k_gain, w_out, prefix_keys, prefix_values, segments, request_group, prefix_owner, mlp_gain, expert_ids, gate_weights, w_gate, w_up, w_down):
    quarters = FF // UNITS
    gate_full = jnp.transpose(w_gate.reshape(EXPERTS, quarters, D, UNITS), (0, 2, 1, 3)).reshape(EXPERTS, D, FF)
    up_full = jnp.transpose(w_up.reshape(EXPERTS, quarters, D, UNITS), (0, 2, 1, 3)).reshape(EXPERTS, D, FF)
    down_full = w_down.reshape(EXPERTS, FF, D)
    tokens_wide = tokens.astype(jnp.float32)
    normed = rms_scale(tokens_wide, attn_gain).astype(jnp.bfloat16)
    projected = jnp.dot(normed, w_qkv.reshape(D, 3 * D), preferred_element_type=jnp.float32).reshape(TOKENS, 3, D)
    queries = rms_scale(projected[:, 0], q_gain).astype(jnp.bfloat16)
    new_keys = rms_scale(projected[:, 1], k_gain).astype(jnp.bfloat16)
    new_values = projected[:, 2].astype(jnp.bfloat16)
    token_group = request_group[segments]
    all_keys = jnp.concatenate([prefix_keys[prefix_owner[group]] for group in range(GROUPS)] + [new_keys], axis=0)
    all_values = jnp.concatenate([prefix_values[prefix_owner[group]] for group in range(GROUPS)] + [new_values], axis=0)
    key_group = jnp.repeat(jnp.arange(GROUPS, dtype=jnp.int32), PREFIX)
    keys_wide = all_keys.astype(jnp.float32).reshape(-1, HEADS, HD)
    values_wide = all_values.astype(jnp.float32).reshape(-1, HEADS, HD)
    positions = jnp.arange(TOKENS, dtype=jnp.int32)

    def attend(block_start):
        block_queries = lax.dynamic_slice_in_dim(queries, block_start, TOK, 0).astype(jnp.float32).reshape(TOK, HEADS, HD)
        block_seg = lax.dynamic_slice_in_dim(segments, block_start, TOK, 0)
        block_group = lax.dynamic_slice_in_dim(token_group, block_start, TOK, 0)
        block_pos = block_start + jnp.arange(TOK, dtype=jnp.int32)
        prefix_mask = block_group[:, None] == key_group[None, :]
        suffix_mask = (block_seg[:, None] == segments[None, :]) & (positions[None, :] <= block_pos[:, None])
        mask = jnp.concatenate([prefix_mask, suffix_mask], axis=1)
        scores = jnp.einsum('qhd,khd->hqk', block_queries, keys_wide, precision=lax.Precision.HIGHEST) * HD ** (-0.5)
        scores = jnp.where(mask[None], scores, -1e+30)
        largest = lax.optimization_barrier(jnp.max(scores, axis=-1, keepdims=True))
        weights = jnp.where(mask[None], jnp.exp(scores - largest), 0.0)
        total = lax.optimization_barrier(jnp.sum(weights, axis=-1))
        rounded = lax.optimization_barrier(weights.astype(jnp.bfloat16))
        mixed = jnp.einsum('hqk,khd->qhd', rounded.astype(jnp.float32), values_wide, precision=lax.Precision.HIGHEST)
        mixed = mixed / jnp.transpose(total)[:, :, None]
        return mixed.astype(jnp.bfloat16).reshape(TOK, D)
    starts = jnp.arange(TOKENS // TOK, dtype=jnp.int32) * TOK
    attended = lax.map(attend, starts).reshape(TOKENS, D)
    attn_sum = jnp.dot(attended, w_out, preferred_element_type=jnp.float32)
    mixed_rows = (tokens_wide + attn_sum).astype(jnp.bfloat16)
    expert_in = rms_scale(mixed_rows.astype(jnp.float32), mlp_gain).astype(jnp.bfloat16)
    blocks = TOKENS // TOK_DEV
    ids_block = expert_ids.reshape(blocks, TOK_DEV * TOP)
    gates_block = gate_weights.reshape(blocks, TOK_DEV * TOP).astype(jnp.float32)
    onehot = (ids_block[:, :, None] == jnp.arange(EXPERTS, dtype=jnp.int32)[None, None, :]).astype(jnp.int32)
    before = jnp.cumsum(onehot, axis=1) - onehot
    position = lax.optimization_barrier(jnp.sum(before * onehot, axis=-1))
    slot = (ids_block * CAP + position).astype(jnp.int32)
    block_rows = jnp.arange(blocks, dtype=jnp.int32)[:, None]
    token_index = (block_rows * TOK_DEV + jnp.arange(TOK_DEV * TOP, dtype=jnp.int32)[None, :] // TOP).astype(jnp.int32)
    token_of_slot = jnp.zeros((blocks, EXPERTS * CAP), jnp.int32).at[block_rows, slot].set(token_index)
    weight_of_slot = jnp.zeros((blocks, EXPERTS * CAP), jnp.float32).at[block_rows, slot].set(gates_block)

    def run_expert(moe_sum, inputs):
        gate_matrix, up_matrix, down_matrix, expert = inputs
        rows = lax.dynamic_slice_in_dim(token_of_slot, expert * CAP, CAP, 1).reshape(-1)
        scale = lax.dynamic_slice_in_dim(weight_of_slot, expert * CAP, CAP, 1).reshape(-1)
        picked = expert_in[rows]
        gated = jnp.dot(picked, gate_matrix, preferred_element_type=jnp.float32)
        upward = jnp.dot(picked, up_matrix, preferred_element_type=jnp.float32)
        activity = (jax.nn.silu(gated) * upward).astype(jnp.bfloat16)
        result = jnp.dot(activity, down_matrix, preferred_element_type=jnp.float32)
        return (moe_sum.at[rows].add(result * scale[:, None]), None)
    moe_init = jnp.zeros((TOKENS, D), jnp.float32)
    moe_sum, _ = lax.scan(run_expert, moe_init, (gate_full, up_full, down_full, jnp.arange(EXPERTS, dtype=jnp.int32)))
    output = (mixed_rows.astype(jnp.float32) + moe_sum).astype(jnp.bfloat16)
    return (output, new_keys, new_values)
```

```python
import functools

import jax
import jax.numpy as jnp
from jax import lax
from jax.experimental import pallas as pl
from jax.experimental.pallas import tpu as pltpu
from jax.sharding import PartitionSpec as P

HD = 128
TOP = 8
EXP_DEV = 2


def from_partner(value, axis, stride):
    mask = 2**stride
    pairs = [(source, source ^ mask) for source in range(lax.axis_size(axis))]
    return lax.ppermute(value, axis, pairs)


def passed_along(value, axis, by):
    devices = lax.axis_size(axis)
    pairs = [(i, i + by) for i in range(devices) if 0 <= i + by < devices]
    return lax.ppermute(value, axis, pairs)


def rms_scale(values, gain):
    mean_square = jnp.mean(values * values, axis=-1, keepdims=True)
    return values * lax.rsqrt(mean_square + 1e-05) * gain.astype(jnp.float32)


def attend_block(carry, queries_heads, block, mask):
    largest, total, accum = carry
    heads_local = queries_heads.shape[1]
    count = block.shape[0]
    key_block = block[:, 0].reshape(count, heads_local, HD)
    value_block = block[:, 1].reshape(count, heads_local, HD)
    scores = jnp.einsum(
        "qhd,khd->hqk", queries_heads, key_block, preferred_element_type=jnp.float32
    ) * HD ** (-0.5)
    scores = jnp.where(mask[None], scores, -1e30)
    new_largest = jnp.maximum(largest, jnp.max(scores, axis=-1))
    weights = jnp.where(mask[None], jnp.exp(scores - new_largest[:, :, None]), 0.0)
    factor = jnp.exp(largest - new_largest)
    total = total * factor + jnp.sum(weights, axis=-1)
    update = jnp.einsum(
        "hqk,khd->hqd",
        weights.astype(jnp.bfloat16),
        value_block,
        preferred_element_type=jnp.float32,
    )
    accum = accum * factor[:, :, None] + update
    return (new_largest, total, accum)


def local(
    tokens,
    attn_gain,
    w_qkv,
    q_gain,
    k_gain,
    w_out,
    prefix_keys,
    prefix_values,
    segments,
    request_group,
    prefix_owner,
    mlp_gain,
    expert_ids,
    gate_weights,
    w_gate,
    w_up,
    w_down,
):
    tensor_size = lax.axis_size("tensor")
    seq_size = lax.axis_size("seq")
    seq_index = lax.axis_index("seq")
    tensor_index = lax.axis_index("tensor")
    tok_dev = tokens.shape[0]
    width = tokens.shape[1]
    tok_seq = tok_dev * tensor_size
    columns = w_qkv.shape[2]
    paired = columns < HD
    normed = rms_scale(tokens.astype(jnp.float32), attn_gain).astype(jnp.bfloat16)
    w_flat = w_qkv.reshape(width, 3 * columns)
    projected = jnp.dot(
        lax.all_gather(normed, "tensor", axis=0, tiled=True),
        w_flat,
        preferred_element_type=jnp.float32,
    )
    query_part = projected[:, :columns]
    key_part = projected[:, columns : 2 * columns]
    squares = lax.psum(
        (jnp.sum(query_part * query_part, axis=-1), jnp.sum(key_part * key_part, axis=-1)), "tensor"
    )
    query_rows = (
        query_part * lax.rsqrt(squares[0] / width + 1e-05)[:, None] * q_gain.astype(jnp.float32)
    ).astype(jnp.bfloat16)
    new_keys = (
        key_part * lax.rsqrt(squares[1] / width + 1e-05)[:, None] * k_gain.astype(jnp.float32)
    ).astype(jnp.bfloat16)
    new_values = projected[:, 2 * columns :].astype(jnp.bfloat16)
    stacked = jnp.stack(
        [
            jnp.concatenate([new_keys, prefix_keys[0]], axis=0),
            jnp.concatenate([new_values, prefix_values[0]], axis=0),
        ],
        axis=1,
    )
    half_rows = tok_seq // 2
    if paired:
        lower_bit = tensor_index % 2
        partner = from_partner(stacked, "tensor", 0)
        full = jnp.where(
            lower_bit == 0,
            jnp.concatenate([stacked, partner], axis=-1),
            jnp.concatenate([partner, stacked], axis=-1),
        )
        query_halves = query_rows.reshape(2, half_rows, columns)
        own_half = lax.dynamic_index_in_dim(query_halves, lower_bit, 0, keepdims=False)
        send_half = lax.dynamic_index_in_dim(query_halves, 1 - lower_bit, 0, keepdims=False)
        got_half = from_partner(send_half, "tensor", 0)
        query_full = jnp.where(
            lower_bit == 0,
            jnp.concatenate([own_half, got_half], axis=-1),
            jnp.concatenate([got_half, own_half], axis=-1),
        )
        query_count = half_rows
        query_offset = lower_bit * half_rows
        heads_local = 1
    else:
        full = stacked
        query_full = query_rows
        query_count = tok_seq
        query_offset = jnp.int32(0)
        heads_local = columns // HD
    suffix_full = full[:tok_seq]
    prefix_full = full[tok_seq:]
    queries_heads = query_full.reshape(query_count, heads_local, HD)
    groups_count = prefix_owner.shape[0]
    request_count = request_group.shape[0]
    token_group = jnp.sum(
        jnp.where(
            segments[:, None] == jnp.arange(request_count, dtype=jnp.int32)[None, :],
            request_group[None, :],
            0,
        ),
        axis=1,
    )
    base_row = seq_index * tok_seq
    query_start = base_row + query_offset
    query_seg = lax.dynamic_slice_in_dim(segments, query_start, query_count, 0)
    query_group = lax.dynamic_slice_in_dim(token_group, query_start, query_count, 0)
    query_pos = query_start + jnp.arange(query_count, dtype=jnp.int32)
    padded_seg = jnp.concatenate([jnp.full((tok_seq,), -1, jnp.int32), segments], axis=0)
    key_seg = lax.dynamic_slice_in_dim(padded_seg, base_row, 2 * tok_seq, 0)
    key_pos = base_row - tok_seq + jnp.arange(2 * tok_seq, dtype=jnp.int32)
    previous = passed_along(suffix_full, "seq", 1)
    suffix_keys = jnp.concatenate([previous, suffix_full], axis=0)
    suffix_mask = (key_seg[None, :] == query_seg[:, None]) & (
        key_pos[None, :] <= query_pos[:, None]
    )
    carry = (
        jnp.full((heads_local, query_count), -1e30, jnp.float32),
        jnp.zeros((heads_local, query_count), jnp.float32),
        jnp.zeros((heads_local, query_count, HD), jnp.float32),
    )
    carry = attend_block(carry, queries_heads, suffix_keys, suffix_mask)
    owner_of_query = jnp.sum(
        jnp.where(
            query_group[:, None] == jnp.arange(groups_count, dtype=jnp.int32)[None, :],
            prefix_owner[None, :],
            0,
        ),
        axis=1,
    )
    state = carry
    piece = lax.all_gather(prefix_full[None], "seq", axis=0, tiled=True)
    start = jnp.int32(0)
    for offset in range(piece.shape[0]):
        slot_mask = (owner_of_query == start + offset)[:, None]
        state = attend_block(state, queries_heads, piece[offset], slot_mask)
    carry = state
    attended = (carry[2] / carry[1][:, :, None]).astype(jnp.bfloat16)
    attended = jnp.transpose(attended, (1, 0, 2)).reshape(query_count, heads_local * HD)
    if paired:
        split_out = attended.reshape(query_count, 2, columns)
        own_out = lax.dynamic_index_in_dim(split_out, lower_bit, 1, keepdims=False)
        send_out = lax.dynamic_index_in_dim(split_out, 1 - lower_bit, 1, keepdims=False)
        got_out = from_partner(send_out, "tensor", 0)
        attended_local = jnp.where(
            lower_bit == 0,
            jnp.concatenate([own_out, got_out], axis=0),
            jnp.concatenate([got_out, own_out], axis=0),
        )
    else:
        attended_local = attended
    attn_sum = lax.psum_scatter(
        jnp.dot(attended_local, w_out, preferred_element_type=jnp.float32).astype(jnp.bfloat16),
        "tensor",
        scatter_dimension=0,
        tiled=True,
    ).astype(jnp.float32)
    mixed_rows = (tokens.astype(jnp.float32) + attn_sum).astype(jnp.bfloat16)
    expert_in = rms_scale(mixed_rows.astype(jnp.float32), mlp_gain).astype(jnp.bfloat16)
    exp_local = EXP_DEV
    experts_all = exp_local * tensor_size
    own_expert = seq_index // (seq_size // exp_local)
    capacity = max(2, 2 * tok_dev * TOP // experts_all)
    flat_ids = expert_ids.reshape(-1)
    onehot = (flat_ids[:, None] == jnp.arange(experts_all, dtype=jnp.int32)[None, :]).astype(
        jnp.int32
    )
    before = jnp.cumsum(onehot, axis=0) - onehot
    slot = flat_ids * capacity + jnp.sum(before * onehot, axis=1)
    slot_match = (
        slot.reshape(tok_dev, TOP)[:, :, None]
        == jnp.arange(experts_all * capacity, dtype=jnp.int32)[None, None, :]
    )
    dispatch_table = jnp.transpose(jnp.any(slot_match, axis=1)).astype(jnp.bfloat16)
    combine_table = jnp.sum(jnp.where(slot_match, gate_weights[:, :, None], 0.0), axis=1)
    buffer = jnp.dot(dispatch_table, expert_in, preferred_element_type=jnp.float32).astype(
        jnp.bfloat16
    )
    buffer = buffer.reshape(tensor_size, exp_local, capacity, width)
    received = lax.all_to_all(buffer, "tensor", split_axis=0, concat_axis=0, tiled=True)
    gate_local = w_gate[0]
    up_local = w_up[0]
    down_local = w_down[0]
    keep_expert = (jnp.arange(exp_local, dtype=jnp.int32) == own_expert)[None, None, :, None, None]
    chosen = lax.dynamic_index_in_dim(
        lax.all_gather(received[None], "seq", axis=0, tiled=True), own_expert, 2, keepdims=False
    )
    gated = jnp.einsum("srcd,df->srcf", chosen, gate_local, preferred_element_type=jnp.float32)
    upward = jnp.einsum("srcd,df->srcf", chosen, up_local, preferred_element_type=jnp.float32)
    activity = (jax.nn.silu(gated) * upward).astype(jnp.bfloat16)
    result = jnp.einsum("srcf,fd->srcd", activity, down_local, preferred_element_type=jnp.float32)
    partials = jnp.where(keep_expert, result[:, :, None], 0.0)
    summed = lax.psum_scatter(
        partials.astype(jnp.bfloat16), "seq", scatter_dimension=0, tiled=True
    ).astype(jnp.float32)
    returned = lax.all_to_all(
        summed[0].astype(jnp.bfloat16), "tensor", split_axis=0, concat_axis=0, tiled=True
    ).astype(jnp.float32)
    moe_sum = jnp.dot(
        combine_table,
        returned.reshape(experts_all * capacity, width),
        preferred_element_type=jnp.float32,
        precision=lax.Precision.HIGHEST,
    )
    output = (mixed_rows.astype(jnp.float32) + moe_sum).astype(jnp.bfloat16)
    return (output, new_keys, new_values)


MESH = pl.DeviceIdType.MESH
F32 = jnp.float32
BF16 = jnp.bfloat16


def pack_rows(value):
    half = value.shape[-1] // 2
    return jnp.concatenate([value[:, :, :half], value[:, :, half:]], axis=1).astype(BF16)


def unpack_rows(value):
    count, rows, half = value.shape
    wide = value.astype(F32).reshape(count, 2, rows // 2, half)
    left = wide[:, 0].reshape(count * (rows // 2), half)
    right = wide[:, 1].reshape(count * (rows // 2), half)
    return jnp.concatenate([left, right], axis=-1)


def layer_kernel(
    dims,
    tokens_ref, attn_gain_ref, q_gain_ref, k_gain_ref, mlp_gain_ref,
    seg_row_ref, cols_ref, ids_ref, gates_ref,
    wqkv_hbm, wout_hbm, pk_hbm, pv_hbm, wg_hbm, wu_hbm, wd_hbm,
    out_ref, keys_ref, values_ref,
    wqkv, wout, pk, pv, wg, wu, wd,
    ag, sq, qkv, att_snd, att_in, rs_snd, rs_in,
    grid_a, grid_b, gate_grid,
    res_a, res_b, rc_a, rc_b, s1_a, s1_b, r1_a, r1_b,
    s2_a, s2_b, r2_a, r2_b, s3_a, s3_b, r3_a, r3_b,
    w_sem,
    ag_ss, ag_rs, sq_ss, sq_rs, qkv_ss, qkv_rs, att_ss, att_rs, rs_ss, rs_rs,
    gg_ss, gg_rs, ga_ss, ga_rs, gb_ss, gb_rs, ra_ss, ra_rs, rb_ss, rb_rs,
):
    S, T, NZ, exp_local = dims
    s = lax.axis_index("seq")
    t = lax.axis_index("tensor")
    x, c = s // 2, s % 2
    z, y = t // 2, t % 2
    tok, width = tokens_ref.shape
    cols = keys_ref.shape[1]
    tok_seq = tok * T
    total_tok = tok_seq * S
    started = []

    loads = [
        pltpu.make_async_copy(wqkv_hbm, wqkv, w_sem.at[0]),
        pltpu.make_async_copy(pk_hbm.at[0], pk, w_sem.at[1]),
        pltpu.make_async_copy(pv_hbm.at[0], pv, w_sem.at[2]),
        pltpu.make_async_copy(wout_hbm, wout, w_sem.at[3]),
        pltpu.make_async_copy(wg_hbm.at[0], wg, w_sem.at[4]),
        pltpu.make_async_copy(wu_hbm.at[0], wu, w_sem.at[5]),
        pltpu.make_async_copy(wd_hbm.at[0], wd, w_sem.at[6]),
    ]
    for load in loads:
        load.start()

    barrier = pltpu.get_barrier_semaphore()
    for k in range(1, T):
        pl.semaphore_signal(barrier, inc=1, device_id=(s, (t + k) % T), device_id_type=MESH)
    for k in range(1, S):
        pl.semaphore_signal(barrier, inc=1, device_id=((s + k) % S, t), device_id_type=MESH)

    def send(src, dst, send_sem, recv_sem, to):
        copy = pltpu.make_async_remote_copy(
            src_ref=src, dst_ref=dst, send_sem=send_sem, recv_sem=recv_sem,
            device_id=to, device_id_type=MESH,
        )
        copy.start()
        started.append(copy)
        return copy

    def to_tensor(k):
        return (s, (t + k) % T)

    def to_seq(k):
        return ((s + k) % S, t)

    peer_x = ((1 - x) * 2 + c, t)
    peer_c = (x * 2 + 1 - c, t)
    peer_y = (s, z * 2 + 1 - y)

    def to_z(k):
        return (s, ((z + k) % NZ) * 2 + y)

    def rms(value, gain):
        mean_square = jnp.mean(value * value, axis=-1, keepdims=True)
        return value * lax.rsqrt(mean_square + 1e-05) * gain

    tokens = tokens_ref[...].astype(F32)
    normed = rms(tokens, attn_gain_ref[...].astype(F32))
    ag[t] = pack_rows(normed[None])[0]
    lane = lax.broadcasted_iota(jnp.int32, (tok, 128), 1)
    dense = jnp.zeros((tok, 128), F32)
    for k in range(ids_ref.shape[1]):
        dense = dense + jnp.where(ids_ref[:, k : k + 1] == lane, gates_ref[:, k : k + 1], 0.0)
    gate_grid[c, x, y, z] = dense
    pl.semaphore_wait(barrier, T + S - 2)
    ag_copies = [
        send(ag.at[t], ag.at[t], ag_ss.at[k], ag_rs.at[k], to_tensor(k)) for k in range(1, T)
    ]
    gg_z = [
        send(gate_grid.at[c, x, y, z], gate_grid.at[c, x, y, z], gg_ss.at[k], gg_rs.at[k], to_z(k))
        for k in range(1, NZ)
    ]
    for copy in ag_copies:
        copy.wait_recv()
    rows = unpack_rows(ag[...]).astype(BF16)
    loads[0].wait()
    proj_q = jnp.dot(rows, wqkv[0], preferred_element_type=F32)
    proj_k = jnp.dot(rows, wqkv[1], preferred_element_type=F32)

    ones = jnp.ones((8, cols), F32)
    nt = (((1,), (1,)), ((), ()))
    squares = jnp.concatenate([proj_q * proj_q, proj_k * proj_k], axis=0)
    sq[t] = lax.dot_general(
        ones, squares, nt, precision=lax.Precision.HIGHEST, preferred_element_type=F32
    )
    sq_copies = [
        send(sq.at[t], sq.at[t], sq_ss.at[k], sq_rs.at[k], to_tensor(k)) for k in range(1, T)
    ]
    for copy in gg_z:
        copy.wait_recv()
    gg_y = send(gate_grid.at[c, x, y], gate_grid.at[c, x, y], gg_ss.at[4], gg_rs.at[4], peer_y)
    proj_v = jnp.dot(rows, wqkv[2], preferred_element_type=F32).astype(BF16)
    values_ref[...] = proj_v
    qkv[s, 2 * tok_seq :] = proj_v
    for copy in sq_copies:
        copy.wait_recv()
    sums = lax.dot_general(
        sq[...].reshape(8 * T, 2 * tok_seq), jnp.full((8 * T, cols), 0.125, F32),
        (((0,), (0,)), ((), ())), precision=lax.Precision.HIGHEST, preferred_element_type=F32,
    )
    inverse = lax.rsqrt(sums / width + 1e-05)
    new_q = (proj_q * inverse[:tok_seq] * q_gain_ref[...].astype(F32)).astype(BF16)
    new_k = (proj_k * inverse[tok_seq:] * k_gain_ref[...].astype(F32)).astype(BF16)
    keys_ref[...] = new_k
    qkv[s, :tok_seq] = new_q
    qkv[s, tok_seq : 2 * tok_seq] = new_k
    qkv_copies = [
        send(qkv.at[s], qkv.at[s], qkv_ss.at[k], qkv_rs.at[k], to_seq(k)) for k in range(1, S)
    ]
    gg_y.wait_recv()
    gg_x = send(gate_grid.at[c, x], gate_grid.at[c, x], gg_ss.at[5], gg_rs.at[5], peer_x)
    for copy in qkv_copies:
        copy.wait_recv()
    loads[1].wait()
    loads[2].wait()

    all_q = qkv[:, :tok_seq].reshape(total_tok, cols)
    all_k = qkv[:, tok_seq : 2 * tok_seq].reshape(total_tok, cols)
    all_v = qkv[:, 2 * tok_seq :].reshape(total_tok, cols)
    pos_q = lax.broadcasted_iota(jnp.int32, (total_tok, total_tok), 0)
    pos_k = lax.broadcasted_iota(jnp.int32, (total_tok, total_tok), 1)
    mask = (cols_ref[:, 0:1] == seg_row_ref[...]) & (pos_k <= pos_q)
    mine = cols_ref[:, 1:2] == s
    heads = []
    for h in range(cols // HD):
        part = slice(h * HD, (h + 1) * HD)
        q_h = all_q[:, part]
        pre = lax.dot_general(q_h, pk[:, part], nt, preferred_element_type=F32) * HD ** (-0.5)
        suf = lax.dot_general(q_h, all_k[:, part], nt, preferred_element_type=F32) * HD ** (-0.5)
        suf = jnp.where(mask, suf, -1e30)
        top = jnp.maximum(
            jnp.max(pre, axis=-1, keepdims=True), jnp.max(suf, axis=-1, keepdims=True)
        )
        pre = jnp.exp(pre - top)
        suf = jnp.where(mask, jnp.exp(suf - top), 0.0)
        total = jnp.sum(pre, axis=-1, keepdims=True) + jnp.sum(suf, axis=-1, keepdims=True)
        mix = jnp.dot(pre.astype(BF16), pv[:, part], preferred_element_type=F32)
        mix = mix + jnp.dot(suf.astype(BF16), all_v[:, part], preferred_element_type=F32)
        heads.append(jnp.where(mine, mix / total, 0.0).astype(BF16))
    att_snd[...] = jnp.concatenate(heads, axis=-1).reshape(S, tok_seq, cols)
    att_copies = [
        send(att_snd.at[(s + k) % S], att_in.at[k], att_ss.at[k], att_rs.at[k], to_seq(k))
        for k in range(1, S)
    ]
    gg_x.wait_recv()
    gg_c = send(gate_grid.at[c], gate_grid.at[c], gg_ss.at[6], gg_rs.at[6], peer_c)
    attended = att_snd[s].astype(F32)
    for k in range(1, S):
        att_copies[k - 1].wait_recv()
        attended = attended + att_in[k].astype(F32)
    loads[3].wait()
    partial = jnp.dot(attended.astype(BF16), wout[...], preferred_element_type=F32)
    rs_snd[...] = pack_rows(partial.reshape(T, tok, width))
    rs_copies = [
        send(rs_snd.at[(t + k) % T], rs_in.at[k], rs_ss.at[k], rs_rs.at[k], to_tensor(k))
        for k in range(1, T)
    ]
    attn_sum = rs_snd[t].astype(F32)
    for k in range(1, T):
        rs_copies[k - 1].wait_recv()
        attn_sum = attn_sum + rs_in[k].astype(F32)
    attn_sum = jnp.concatenate([attn_sum[:tok], attn_sum[tok:]], axis=-1)
    mixed = (tokens + attn_sum).astype(BF16).astype(F32)
    expert_in = rms(mixed, mlp_gain_ref[...].astype(F32))

    half = width // 2
    grid_a[c, x, y, z] = pack_rows(expert_in[None, :, :half])[0]
    grid_b[c, y, x, z] = pack_rows(expert_in[None, :, half:])[0]
    mine_a, mine_b = grid_a.at[c, x, y, z], grid_b.at[c, y, x, z]
    z_a = [send(mine_a, mine_a, ga_ss.at[k], ga_rs.at[k], to_z(k)) for k in range(1, NZ)]
    z_b = [send(mine_b, mine_b, gb_ss.at[k], gb_rs.at[k], to_z(k)) for k in range(1, NZ)]
    for copy in z_a:
        copy.wait_recv()
    two_a = send(grid_a.at[c, x, y], grid_a.at[c, x, y], ga_ss.at[4], ga_rs.at[4], peer_y)
    for copy in z_b:
        copy.wait_recv()
    two_b = send(grid_b.at[c, y, x], grid_b.at[c, y, x], gb_ss.at[4], gb_rs.at[4], peer_x)
    two_a.wait_recv()
    one_a = send(grid_a.at[c, x], grid_a.at[c, x], ga_ss.at[5], ga_rs.at[5], peer_x)
    two_b.wait_recv()
    one_b = send(grid_b.at[c, y], grid_b.at[c, y], gb_ss.at[5], gb_rs.at[5], peer_y)
    one_a.wait_recv()
    core_a = send(grid_a.at[c], grid_a.at[c], ga_ss.at[6], ga_rs.at[6], peer_c)
    one_b.wait_recv()
    core_b = send(grid_b.at[c], grid_b.at[c], gb_ss.at[6], gb_rs.at[6], peer_c)
    for load in loads[4:]:
        load.wait()
    gg_c.wait_recv()
    expert = exp_local * t + s // (S // exp_local)
    blocks = 4 * NZ

    def run_half(side):
        block_a = grid_a[side].reshape(blocks, 2 * tok, half // 2)
        raw_b = grid_b[side]
        block_b = jnp.concatenate([raw_b[j, i] for i in range(2) for j in range(2)], axis=0)
        inputs = jnp.concatenate([unpack_rows(block_a), unpack_rows(block_b)], axis=-1).astype(BF16)
        gated = jnp.dot(inputs, wg[...], preferred_element_type=F32)
        upward = jnp.dot(inputs, wu[...], preferred_element_type=F32)
        act = (gated / (1.0 + jnp.exp(-gated)) * upward).astype(BF16)
        result = jnp.dot(act, wd[...], preferred_element_type=F32)
        table = gate_grid[side].reshape(blocks * tok, 128)
        lanes = lax.broadcasted_iota(jnp.int32, table.shape, 1)
        scale = jnp.sum(jnp.where(lanes == expert, table, 0.0), axis=-1, keepdims=True)
        result = (result * scale).reshape(blocks, tok, width)
        res_a[side] = pack_rows(result[:, :, :half]).reshape(2, 2, NZ, 2 * tok, half // 2)
        packed_b = pack_rows(result[:, :, half:])
        for i in range(2):
            for j in range(2):
                first = (i * 2 + j) * NZ
                res_b[side, j, i] = packed_b[first : first + NZ]

    core_a.wait_recv()
    core_b.wait_recv()
    run_half(1 - c)
    rcore_a = send(res_a.at[1 - c], rc_a, ra_ss.at[0], ra_rs.at[0], peer_c)
    rcore_b = send(res_b.at[1 - c], rc_b, rb_ss.at[0], rb_rs.at[0], peer_c)
    run_half(c)

    def added(first, second):
        return (first.astype(F32) + second.astype(F32)).astype(BF16)

    rcore_a.wait_recv()
    s1_a[...] = added(res_a[c], rc_a[...])
    rone_a = send(s1_a.at[1 - x], r1_a, ra_ss.at[1], ra_rs.at[1], peer_x)
    rcore_b.wait_recv()
    s1_b[...] = added(res_b[c], rc_b[...])
    rone_b = send(s1_b.at[1 - y], r1_b, rb_ss.at[1], rb_rs.at[1], peer_y)
    rone_b.wait_recv()
    s2_b[...] = added(s1_b[y], r1_b[...])
    rone_a.wait_recv()
    s2_a[...] = added(s1_a[x], r1_a[...])
    rtwo_a = send(s2_a.at[1 - y], r2_a, ra_ss.at[2], ra_rs.at[2], peer_y)
    rtwo_b = send(s2_b.at[1 - x], r2_b, rb_ss.at[2], rb_rs.at[2], peer_x)
    rtwo_a.wait_recv()
    s3_a[...] = added(s2_a[y], r2_a[...])
    rz_a = [
        send(s3_a.at[(z + k) % NZ], r3_a.at[k], ra_ss.at[2 + k], ra_rs.at[2 + k], to_z(k))
        for k in range(1, NZ)
    ]
    rtwo_b.wait_recv()
    s3_b[...] = added(s2_b[x], r2_b[...])
    rz_b = [
        send(s3_b.at[(z + k) % NZ], r3_b.at[k], rb_ss.at[2 + k], rb_rs.at[2 + k], to_z(k))
        for k in range(1, NZ)
    ]
    sum_a = s3_a[z].astype(F32)
    sum_b = s3_b[z].astype(F32)
    for k in range(1, NZ):
        rz_a[k - 1].wait_recv()
        sum_a = sum_a + r3_a[k].astype(F32)
    for k in range(1, NZ):
        rz_b[k - 1].wait_recv()
        sum_b = sum_b + r3_b[k].astype(F32)
    moe = jnp.concatenate([sum_a[:tok], sum_a[tok:], sum_b[:tok], sum_b[tok:]], axis=-1)
    out_ref[...] = (mixed + moe).astype(BF16)
    for copy in started:
        copy.wait_send()


def local_kernel(
    tokens, attn_gain, w_qkv, q_gain, k_gain, w_out, prefix_keys, prefix_values, segments,
    request_group, prefix_owner, mlp_gain, expert_ids, gate_weights, w_gate, w_up, w_down,
):
    S, T = lax.axis_size("seq"), lax.axis_size("tensor")
    NZ = T // 2
    tok, width = tokens.shape
    cols = w_qkv.shape[2]
    tok_seq = tok * T
    slots = prefix_keys.shape[1]
    units = w_gate.shape[2]
    request = jnp.arange(request_group.shape[0], dtype=jnp.int32)
    group = jnp.arange(prefix_owner.shape[0], dtype=jnp.int32)
    owner_of_request = jnp.sum(
        jnp.where(request_group[:, None] == group[None, :], prefix_owner[None, :], 0), axis=1
    )
    owner = jnp.sum(
        jnp.where(segments[:, None] == request[None, :], owner_of_request[None, :], 0), axis=1
    )
    columns = jnp.stack([segments, owner], axis=1)
    vm, dma = pltpu.VMEM, pltpu.SemaphoreType.DMA
    quarter = width // 4
    blk = (2 * tok, quarter)
    grid = vm((2, 2, 2, NZ) + blk, BF16)
    pair = lambda *lead: [vm(lead + blk, BF16)] * 2
    scratch = [
        vm((3, width, cols), BF16), vm((cols, width), BF16),
        vm((slots, cols), BF16), vm((slots, cols), BF16),
        vm((width, units), BF16), vm((width, units), BF16), vm((units, width), BF16),
        vm((T, 2 * tok, width // 2), BF16), vm((T, 8, 2 * tok_seq), F32),
        vm((S, 3 * tok_seq, cols), BF16), vm((S, tok_seq, cols), BF16), vm((S, tok_seq, cols), BF16),
        vm((T, 2 * tok, width // 2), BF16), vm((T, 2 * tok, width // 2), BF16),
        grid, grid, vm((2, 2, 2, NZ, tok, 128), F32),
        grid, grid,
        *pair(2, 2, NZ), *pair(2, 2, NZ), *pair(2, NZ),
        *pair(2, NZ), *pair(NZ), *pair(NZ), *pair(NZ),
        dma((7,)),
        *[dma((T,))] * 4, *[dma((S,))] * 4, *[dma((T,))] * 2,
        *[dma((8,))] * 10,
    ]
    in_vmem = pl.BlockSpec(memory_space=pltpu.VMEM)
    in_any = pl.BlockSpec(memory_space=pl.ANY)
    return pl.pallas_call(
        functools.partial(layer_kernel, (S, T, NZ, EXP_DEV)),
        out_shape=(
            jax.ShapeDtypeStruct((tok, width), BF16),
            jax.ShapeDtypeStruct((tok_seq, cols), BF16),
            jax.ShapeDtypeStruct((tok_seq, cols), BF16),
        ),
        in_specs=[in_vmem] * 9 + [in_any] * 7,
        out_specs=(in_vmem,) * 3,
        scratch_shapes=scratch,
        compiler_params=pltpu.CompilerParams(
            collective_id=0, has_side_effects=True, vmem_limit_bytes=56 * 2**20
        ),
    )(
        tokens, attn_gain[None], q_gain[None], k_gain[None], mlp_gain[None],
        segments[None], columns, expert_ids, gate_weights,
        jnp.transpose(w_qkv, (1, 0, 2)), w_out, prefix_keys, prefix_values, w_gate, w_up, w_down,
    )


def whole_heads(*arrays):
    seq_size, tensor_size = lax.axis_size("seq"), lax.axis_size("tensor")
    if arrays[2].shape[2] % HD == 0 and seq_size == 4 and tensor_size == 8:
        return local_kernel(*arrays)
    return local(*arrays)


def solution(mesh):
    return jax.shard_map(
        whole_heads,
        mesh=mesh,
        in_specs=(
            P(("seq", "tensor"), None),
            P(),
            P(None, None, "tensor"),
            P("tensor"),
            P("tensor"),
            P("tensor", None),
            P("seq", None, "tensor"),
            P("seq", None, "tensor"),
            P(),
            P(),
            P(),
            P(),
            P(("seq", "tensor"), None),
            P(("seq", "tensor"), None),
            P(("tensor", "seq"), None, None),
            P(("tensor", "seq"), None, None),
            P(("tensor", "seq"), None, None),
        ),
        out_specs=(P(("seq", "tensor"), None), P("seq", "tensor"), P("seq", "tensor")),
        check_vma=False,
    )
```

```python
import functools

import jax
import jax.numpy as jnp
from jax import lax
from jax.experimental import pallas as pl
from jax.experimental.pallas import tpu as pltpu
from jax.sharding import PartitionSpec as P

HD = 128
TOP = 8
EXP_DEV = 2


def from_partner(value, axis, stride):
    mask = 2**stride
    pairs = [(source, source ^ mask) for source in range(lax.axis_size(axis))]
    return lax.ppermute(value, axis, pairs)


def passed_along(value, axis, by):
    devices = lax.axis_size(axis)
    pairs = [(i, i + by) for i in range(devices) if 0 <= i + by < devices]
    return lax.ppermute(value, axis, pairs)


def rms_scale(values, gain):
    mean_square = jnp.mean(values * values, axis=-1, keepdims=True)
    return values * lax.rsqrt(mean_square + 1e-05) * gain.astype(jnp.float32)


def attend_block(carry, queries_heads, block, mask):
    largest, total, accum = carry
    heads_local = queries_heads.shape[1]
    count = block.shape[0]
    key_block = block[:, 0].reshape(count, heads_local, HD)
    value_block = block[:, 1].reshape(count, heads_local, HD)
    scores = jnp.einsum(
        "qhd,khd->hqk", queries_heads, key_block, preferred_element_type=jnp.float32
    ) * HD ** (-0.5)
    scores = jnp.where(mask[None], scores, -1e30)
    new_largest = jnp.maximum(largest, jnp.max(scores, axis=-1))
    weights = jnp.where(mask[None], jnp.exp(scores - new_largest[:, :, None]), 0.0)
    factor = jnp.exp(largest - new_largest)
    total = total * factor + jnp.sum(weights, axis=-1)
    update = jnp.einsum(
        "hqk,khd->hqd",
        weights.astype(jnp.bfloat16),
        value_block,
        preferred_element_type=jnp.float32,
    )
    accum = accum * factor[:, :, None] + update
    return (new_largest, total, accum)


def local(
    tokens,
    attn_gain,
    w_qkv,
    q_gain,
    k_gain,
    w_out,
    prefix_keys,
    prefix_values,
    segments,
    request_group,
    prefix_owner,
    mlp_gain,
    expert_ids,
    gate_weights,
    w_gate,
    w_up,
    w_down,
):
    tensor_size = lax.axis_size("tensor")
    seq_size = lax.axis_size("seq")
    seq_index = lax.axis_index("seq")
    tensor_index = lax.axis_index("tensor")
    tok_dev = tokens.shape[0]
    width = tokens.shape[1]
    tok_seq = tok_dev * tensor_size
    columns = w_qkv.shape[2]
    paired = columns < HD
    normed = rms_scale(tokens.astype(jnp.float32), attn_gain).astype(jnp.bfloat16)
    w_flat = w_qkv.reshape(width, 3 * columns)
    projected = jnp.dot(
        lax.all_gather(normed, "tensor", axis=0, tiled=True),
        w_flat,
        preferred_element_type=jnp.float32,
    )
    query_part = projected[:, :columns]
    key_part = projected[:, columns : 2 * columns]
    squares = lax.psum(
        (jnp.sum(query_part * query_part, axis=-1), jnp.sum(key_part * key_part, axis=-1)), "tensor"
    )
    query_rows = (
        query_part * lax.rsqrt(squares[0] / width + 1e-05)[:, None] * q_gain.astype(jnp.float32)
    ).astype(jnp.bfloat16)
    new_keys = (
        key_part * lax.rsqrt(squares[1] / width + 1e-05)[:, None] * k_gain.astype(jnp.float32)
    ).astype(jnp.bfloat16)
    new_values = projected[:, 2 * columns :].astype(jnp.bfloat16)
    stacked = jnp.stack(
        [
            jnp.concatenate([new_keys, prefix_keys[0]], axis=0),
            jnp.concatenate([new_values, prefix_values[0]], axis=0),
        ],
        axis=1,
    )
    half_rows = tok_seq // 2
    if paired:
        lower_bit = tensor_index % 2
        partner = from_partner(stacked, "tensor", 0)
        full = jnp.where(
            lower_bit == 0,
            jnp.concatenate([stacked, partner], axis=-1),
            jnp.concatenate([partner, stacked], axis=-1),
        )
        query_halves = query_rows.reshape(2, half_rows, columns)
        own_half = lax.dynamic_index_in_dim(query_halves, lower_bit, 0, keepdims=False)
        send_half = lax.dynamic_index_in_dim(query_halves, 1 - lower_bit, 0, keepdims=False)
        got_half = from_partner(send_half, "tensor", 0)
        query_full = jnp.where(
            lower_bit == 0,
            jnp.concatenate([own_half, got_half], axis=-1),
            jnp.concatenate([got_half, own_half], axis=-1),
        )
        query_count = half_rows
        query_offset = lower_bit * half_rows
        heads_local = 1
    else:
        full = stacked
        query_full = query_rows
        query_count = tok_seq
        query_offset = jnp.int32(0)
        heads_local = columns // HD
    suffix_full = full[:tok_seq]
    prefix_full = full[tok_seq:]
    queries_heads = query_full.reshape(query_count, heads_local, HD)
    groups_count = prefix_owner.shape[0]
    request_count = request_group.shape[0]
    token_group = jnp.sum(
        jnp.where(
            segments[:, None] == jnp.arange(request_count, dtype=jnp.int32)[None, :],
            request_group[None, :],
            0,
        ),
        axis=1,
    )
    base_row = seq_index * tok_seq
    query_start = base_row + query_offset
    query_seg = lax.dynamic_slice_in_dim(segments, query_start, query_count, 0)
    query_group = lax.dynamic_slice_in_dim(token_group, query_start, query_count, 0)
    query_pos = query_start + jnp.arange(query_count, dtype=jnp.int32)
    padded_seg = jnp.concatenate([jnp.full((tok_seq,), -1, jnp.int32), segments], axis=0)
    key_seg = lax.dynamic_slice_in_dim(padded_seg, base_row, 2 * tok_seq, 0)
    key_pos = base_row - tok_seq + jnp.arange(2 * tok_seq, dtype=jnp.int32)
    previous = passed_along(suffix_full, "seq", 1)
    suffix_keys = jnp.concatenate([previous, suffix_full], axis=0)
    suffix_mask = (key_seg[None, :] == query_seg[:, None]) & (
        key_pos[None, :] <= query_pos[:, None]
    )
    carry = (
        jnp.full((heads_local, query_count), -1e30, jnp.float32),
        jnp.zeros((heads_local, query_count), jnp.float32),
        jnp.zeros((heads_local, query_count, HD), jnp.float32),
    )
    carry = attend_block(carry, queries_heads, suffix_keys, suffix_mask)
    owner_of_query = jnp.sum(
        jnp.where(
            query_group[:, None] == jnp.arange(groups_count, dtype=jnp.int32)[None, :],
            prefix_owner[None, :],
            0,
        ),
        axis=1,
    )
    state = carry
    piece = lax.all_gather(prefix_full[None], "seq", axis=0, tiled=True)
    start = jnp.int32(0)
    for offset in range(piece.shape[0]):
        slot_mask = (owner_of_query == start + offset)[:, None]
        state = attend_block(state, queries_heads, piece[offset], slot_mask)
    carry = state
    attended = (carry[2] / carry[1][:, :, None]).astype(jnp.bfloat16)
    attended = jnp.transpose(attended, (1, 0, 2)).reshape(query_count, heads_local * HD)
    if paired:
        split_out = attended.reshape(query_count, 2, columns)
        own_out = lax.dynamic_index_in_dim(split_out, lower_bit, 1, keepdims=False)
        send_out = lax.dynamic_index_in_dim(split_out, 1 - lower_bit, 1, keepdims=False)
        got_out = from_partner(send_out, "tensor", 0)
        attended_local = jnp.where(
            lower_bit == 0,
            jnp.concatenate([own_out, got_out], axis=0),
            jnp.concatenate([got_out, own_out], axis=0),
        )
    else:
        attended_local = attended
    attn_sum = lax.psum_scatter(
        jnp.dot(attended_local, w_out, preferred_element_type=jnp.float32).astype(jnp.bfloat16),
        "tensor",
        scatter_dimension=0,
        tiled=True,
    ).astype(jnp.float32)
    mixed_rows = (tokens.astype(jnp.float32) + attn_sum).astype(jnp.bfloat16)
    expert_in = rms_scale(mixed_rows.astype(jnp.float32), mlp_gain).astype(jnp.bfloat16)
    exp_local = EXP_DEV
    experts_all = exp_local * tensor_size
    own_expert = seq_index // (seq_size // exp_local)
    capacity = max(2, 2 * tok_dev * TOP // experts_all)
    flat_ids = expert_ids.reshape(-1)
    onehot = (flat_ids[:, None] == jnp.arange(experts_all, dtype=jnp.int32)[None, :]).astype(
        jnp.int32
    )
    before = jnp.cumsum(onehot, axis=0) - onehot
    slot = flat_ids * capacity + jnp.sum(before * onehot, axis=1)
    slot_match = (
        slot.reshape(tok_dev, TOP)[:, :, None]
        == jnp.arange(experts_all * capacity, dtype=jnp.int32)[None, None, :]
    )
    dispatch_table = jnp.transpose(jnp.any(slot_match, axis=1)).astype(jnp.bfloat16)
    combine_table = jnp.sum(jnp.where(slot_match, gate_weights[:, :, None], 0.0), axis=1)
    buffer = jnp.dot(dispatch_table, expert_in, preferred_element_type=jnp.float32).astype(
        jnp.bfloat16
    )
    buffer = buffer.reshape(tensor_size, exp_local, capacity, width)
    received = lax.all_to_all(buffer, "tensor", split_axis=0, concat_axis=0, tiled=True)
    gate_local = w_gate[0]
    up_local = w_up[0]
    down_local = w_down[0]
    keep_expert = (jnp.arange(exp_local, dtype=jnp.int32) == own_expert)[None, None, :, None, None]
    chosen = lax.dynamic_index_in_dim(
        lax.all_gather(received[None], "seq", axis=0, tiled=True), own_expert, 2, keepdims=False
    )
    gated = jnp.einsum("srcd,df->srcf", chosen, gate_local, preferred_element_type=jnp.float32)
    upward = jnp.einsum("srcd,df->srcf", chosen, up_local, preferred_element_type=jnp.float32)
    activity = (jax.nn.silu(gated) * upward).astype(jnp.bfloat16)
    result = jnp.einsum("srcf,fd->srcd", activity, down_local, preferred_element_type=jnp.float32)
    partials = jnp.where(keep_expert, result[:, :, None], 0.0)
    summed = lax.psum_scatter(
        partials.astype(jnp.bfloat16), "seq", scatter_dimension=0, tiled=True
    ).astype(jnp.float32)
    returned = lax.all_to_all(
        summed[0].astype(jnp.bfloat16), "tensor", split_axis=0, concat_axis=0, tiled=True
    ).astype(jnp.float32)
    moe_sum = jnp.dot(
        combine_table,
        returned.reshape(experts_all * capacity, width),
        preferred_element_type=jnp.float32,
        precision=lax.Precision.HIGHEST,
    )
    output = (mixed_rows.astype(jnp.float32) + moe_sum).astype(jnp.bfloat16)
    return (output, new_keys, new_values)


MESH = pl.DeviceIdType.MESH
F32 = jnp.float32
BF16 = jnp.bfloat16


def pack_rows(value):
    half = value.shape[-1] // 2
    return jnp.concatenate([value[:, :, :half], value[:, :, half:]], axis=1).astype(BF16)


def unpack_rows(value):
    count, rows, half = value.shape
    wide = value.astype(F32).reshape(count, 2, rows // 2, half)
    left = wide[:, 0].reshape(count * (rows // 2), half)
    right = wide[:, 1].reshape(count * (rows // 2), half)
    return jnp.concatenate([left, right], axis=-1)


def layer_kernel(
    dims,
    tokens_ref, attn_gain_ref, q_gain_ref, k_gain_ref, mlp_gain_ref,
    seg_row_ref, request_ref, slot_ref, ids_ref, gates_ref,
    wqkv_hbm, wout_hbm, pk_hbm, pv_hbm, wg_hbm, wu_hbm, wd_hbm,
    out_ref, keys_ref, values_ref,
    wqkv, wout, pk, pv, wg, wu, wd,
    ag, sq, sums_grid, qv, ks, att_snd, att_in, rs_snd, rs_in,
    grid_a, grid_b, gate_grid,
    res_a, res_b, rc_a, rc_b, s1_a, s1_b, r1_a, r1_b,
    s2_a, s2_b, r2_a, r2_b, s3_a, s3_b, r3_a, r3_b,
    w_sem,
    ag_ss, ag_rs, sq_ss, sq_rs, qv_ss, qv_rs, ks_ss, ks_rs, sm_ss, sm_rs, att_ss, att_rs, rs_ss, rs_rs,
    gg_ss, gg_rs, ga_ss, ga_rs, gb_ss, gb_rs, ra_ss, ra_rs, rb_ss, rb_rs,
):
    S, T, NZ, exp_local = dims
    s = lax.axis_index("seq")
    t = lax.axis_index("tensor")
    x, c = s // 2, s % 2
    z, y = t // 2, t % 2
    tok, width = tokens_ref.shape
    cols = keys_ref.shape[1]
    tok_seq = tok * T
    total_tok = tok_seq * S
    started = []

    loads = [
        pltpu.make_async_copy(wqkv_hbm, wqkv, w_sem.at[0]),
        pltpu.make_async_copy(pk_hbm.at[0], pk, w_sem.at[1]),
        pltpu.make_async_copy(pv_hbm.at[0], pv, w_sem.at[2]),
        pltpu.make_async_copy(wout_hbm, wout, w_sem.at[3]),
        pltpu.make_async_copy(wg_hbm.at[0], wg, w_sem.at[4]),
        pltpu.make_async_copy(wu_hbm.at[0], wu, w_sem.at[5]),
        pltpu.make_async_copy(wd_hbm.at[0], wd, w_sem.at[6]),
    ]
    for load in loads:
        load.start()

    barrier = pltpu.get_barrier_semaphore()
    for k in range(1, T):
        pl.semaphore_signal(barrier, inc=1, device_id=(s, (t + k) % T), device_id_type=MESH)
    for k in range(1, S):
        pl.semaphore_signal(barrier, inc=1, device_id=((s + k) % S, t), device_id_type=MESH)

    def send(src, dst, send_sem, recv_sem, to):
        copy = pltpu.make_async_remote_copy(
            src_ref=src, dst_ref=dst, send_sem=send_sem, recv_sem=recv_sem,
            device_id=to, device_id_type=MESH,
        )
        copy.start()
        started.append(copy)
        return copy

    def to_tensor(k):
        return (s, (t + k) % T)

    def to_seq(k):
        return ((s + k) % S, t)

    peer_x = ((1 - x) * 2 + c, t)
    peer_c = (x * 2 + 1 - c, t)
    peer_y = (s, z * 2 + 1 - y)

    def to_z(k):
        return (s, ((z + k) % NZ) * 2 + y)

    def rms(value, gain):
        mean_square = jnp.mean(value * value, axis=-1, keepdims=True)
        return value * lax.rsqrt(mean_square + 1e-05) * gain

    tokens = tokens_ref[...].astype(F32)
    normed = rms(tokens, attn_gain_ref[...].astype(F32).reshape(1, width))
    ag[t] = pack_rows(normed[None])[0]
    lane = lax.broadcasted_iota(jnp.int32, (tok, 128), 1)
    dense = jnp.zeros((tok, 128), F32)
    for k in range(ids_ref.shape[1]):
        dense = dense + jnp.where(ids_ref[:, k : k + 1] == lane, gates_ref[:, k : k + 1], 0.0)
    gate_grid[c, x, y, z] = dense
    pl.semaphore_wait(barrier, T + S - 2)
    ag_copies = [
        send(ag.at[t], ag.at[t], ag_ss.at[k], ag_rs.at[k], to_tensor(k)) for k in range(1, T)
    ]
    gg_z = [
        send(gate_grid.at[c, x, y, z], gate_grid.at[c, x, y, z], gg_ss.at[k], gg_rs.at[k], to_z(k))
        for k in range(1, NZ)
    ]
    for copy in ag_copies:
        copy.wait_recv()
    rows = unpack_rows(ag[...]).astype(BF16)
    loads[0].wait()
    proj_q = jnp.dot(rows, wqkv[0], preferred_element_type=F32)
    proj_k = jnp.dot(rows, wqkv[1], preferred_element_type=F32)

    ones = jnp.ones((8, cols), F32)
    nt = (((1,), (1,)), ((), ()))
    squares = jnp.concatenate([proj_q * proj_q, proj_k * proj_k], axis=0)
    sq[t] = lax.dot_general(
        ones, squares, nt, precision=lax.Precision.HIGHEST, preferred_element_type=F32
    )
    sq_copies = [
        send(sq.at[t], sq.at[t], sq_ss.at[k], sq_rs.at[k], to_tensor(k)) for k in range(1, T)
    ]
    for copy in gg_z:
        copy.wait_recv()
    gg_y = send(gate_grid.at[c, x, y], gate_grid.at[c, x, y], gg_ss.at[4], gg_rs.at[4], peer_y)
    proj_v = jnp.dot(rows, wqkv[2], preferred_element_type=F32).astype(BF16)
    values_ref[...] = proj_v
    qv[s, :tok_seq] = (proj_q * q_gain_ref[...].astype(F32).reshape(1, cols)).astype(BF16)
    qv[s, tok_seq:] = proj_v
    qv_copies = [send(qv.at[s], qv.at[s], qv_ss.at[k], qv_rs.at[k], to_seq(k)) for k in range(1, S)]
    for copy in sq_copies:
        copy.wait_recv()
    sums_row = sq[0]
    for k in range(1, T):
        sums_row = sums_row + sq[k]
    sums_grid[s] = sums_row
    sums_copies = [
        send(sums_grid.at[s], sums_grid.at[s], sm_ss.at[k], sm_rs.at[k], to_seq(k))
        for k in range(1, S)
    ]

    def inverse_columns(sums):
        turned = lax.dot_general(
            sums, jnp.full((8, 128), 0.125, F32), (((0,), (0,)), ((), ())),
            precision=lax.Precision.HIGHEST, preferred_element_type=F32,
        )
        return lax.rsqrt(turned / width + 1e-05)[:, :1]

    new_k = (
        proj_k * inverse_columns(sums_row)[tok_seq:] * k_gain_ref[...].astype(F32).reshape(1, cols)
    ).astype(BF16)
    keys_ref[...] = new_k
    ks[s] = new_k
    ks_copies = [send(ks.at[s], ks.at[s], ks_ss.at[k], ks_rs.at[k], to_seq(k)) for k in range(1, S)]
    gg_y.wait_recv()
    gg_x = send(gate_grid.at[c, x], gate_grid.at[c, x], gg_ss.at[5], gg_rs.at[5], peer_x)
    pos_q = lax.broadcasted_iota(jnp.int32, (total_tok, total_tok), 0)
    pos_k = lax.broadcasted_iota(jnp.int32, (total_tok, total_tok), 1)

    def as_column(row):
        wide = jnp.where(pos_q == pos_k, row.astype(F32), 0.0)
        return jnp.sum(wide, axis=-1, keepdims=True).astype(jnp.int32)

    seg_row = seg_row_ref[...]
    owner_row = jnp.zeros(seg_row.shape, jnp.int32)
    for r in range(request_ref.shape[0]):
        slot = jnp.int32(0)
        for g in range(slot_ref.shape[0]):
            slot = jnp.where(request_ref[r] == g, slot_ref[g], slot)
        owner_row = jnp.where(seg_row == r, slot, owner_row)
    mask = (as_column(seg_row) == seg_row) & (pos_k <= pos_q)
    mine = as_column(owner_row) == s
    loads[1].wait()
    loads[2].wait()
    for copy in qv_copies + sums_copies + ks_copies:
        copy.wait_recv()

    all_q = qv[:, :tok_seq].reshape(total_tok, cols)
    all_v = qv[:, tok_seq:].reshape(total_tok, cols)
    all_k = ks[...].reshape(total_tok, cols)
    scale_q = jnp.concatenate([inverse_columns(sums_grid[k])[:tok_seq] for k in range(S)], axis=0)
    scale_q = scale_q * HD ** (-0.5)
    heads = []
    for h in range(cols // HD):
        part = slice(h * HD, (h + 1) * HD)
        q_h = all_q[:, part]
        pre = lax.dot_general(q_h, pk[:, part], nt, preferred_element_type=F32) * scale_q
        suf = lax.dot_general(q_h, all_k[:, part], nt, preferred_element_type=F32) * scale_q
        suf = jnp.where(mask, suf, -1e30)
        top = jnp.maximum(
            jnp.max(pre, axis=-1, keepdims=True), jnp.max(suf, axis=-1, keepdims=True)
        )
        pre = jnp.exp(pre - top)
        suf = jnp.where(mask, jnp.exp(suf - top), 0.0)
        total = jnp.sum(pre, axis=-1, keepdims=True) + jnp.sum(suf, axis=-1, keepdims=True)
        mix = jnp.dot(pre.astype(BF16), pv[:, part], preferred_element_type=F32)
        mix = mix + jnp.dot(suf.astype(BF16), all_v[:, part], preferred_element_type=F32)
        heads.append(jnp.where(mine, mix / total, 0.0).astype(BF16))
    att_snd[...] = jnp.concatenate(heads, axis=-1).reshape(S, tok_seq, cols)
    att_copies = [
        send(att_snd.at[(s + k) % S], att_in.at[k], att_ss.at[k], att_rs.at[k], to_seq(k))
        for k in range(1, S)
    ]
    gg_x.wait_recv()
    gg_c = send(gate_grid.at[c], gate_grid.at[c], gg_ss.at[6], gg_rs.at[6], peer_c)
    attended = att_snd[s].astype(F32)
    for k in range(1, S):
        att_copies[k - 1].wait_recv()
        attended = attended + att_in[k].astype(F32)
    loads[3].wait()
    partial = jnp.dot(attended.astype(BF16), wout[...], preferred_element_type=F32)
    rs_snd[...] = pack_rows(partial.reshape(T, tok, width))
    rs_copies = [
        send(rs_snd.at[(t + k) % T], rs_in.at[k], rs_ss.at[k], rs_rs.at[k], to_tensor(k))
        for k in range(1, T)
    ]
    attn_sum = rs_snd[t].astype(F32)
    for k in range(1, T):
        rs_copies[k - 1].wait_recv()
        attn_sum = attn_sum + rs_in[k].astype(F32)
    attn_sum = jnp.concatenate([attn_sum[:tok], attn_sum[tok:]], axis=-1)
    mixed = (tokens + attn_sum).astype(BF16).astype(F32)
    expert_in = rms(mixed, mlp_gain_ref[...].astype(F32).reshape(1, width))

    half = width // 2
    grid_a[c, x, y, z] = pack_rows(expert_in[None, :, :half])[0]
    grid_b[c, y, x, z] = pack_rows(expert_in[None, :, half:])[0]
    mine_a, mine_b = grid_a.at[c, x, y, z], grid_b.at[c, y, x, z]
    z_a = [send(mine_a, mine_a, ga_ss.at[k], ga_rs.at[k], to_z(k)) for k in range(1, NZ)]
    z_b = [send(mine_b, mine_b, gb_ss.at[k], gb_rs.at[k], to_z(k)) for k in range(1, NZ)]
    for copy in z_a:
        copy.wait_recv()
    two_a = send(grid_a.at[c, x, y], grid_a.at[c, x, y], ga_ss.at[4], ga_rs.at[4], peer_y)
    for copy in z_b:
        copy.wait_recv()
    two_b = send(grid_b.at[c, y, x], grid_b.at[c, y, x], gb_ss.at[4], gb_rs.at[4], peer_x)
    two_a.wait_recv()
    one_a = send(grid_a.at[c, x], grid_a.at[c, x], ga_ss.at[5], ga_rs.at[5], peer_x)
    two_b.wait_recv()
    one_b = send(grid_b.at[c, y], grid_b.at[c, y], gb_ss.at[5], gb_rs.at[5], peer_y)
    one_a.wait_recv()
    core_a = send(grid_a.at[c], grid_a.at[c], ga_ss.at[6], ga_rs.at[6], peer_c)
    one_b.wait_recv()
    core_b = send(grid_b.at[c], grid_b.at[c], gb_ss.at[6], gb_rs.at[6], peer_c)
    for load in loads[4:]:
        load.wait()
    gg_c.wait_recv()
    expert = exp_local * t + s // (S // exp_local)
    blocks = 4 * NZ

    def activity(side):
        block_a = grid_a[side].reshape(blocks, 2 * tok, half // 2)
        raw_b = grid_b[side]
        block_b = jnp.concatenate([raw_b[j, i] for i in range(2) for j in range(2)], axis=0)
        inputs = jnp.concatenate([unpack_rows(block_a), unpack_rows(block_b)], axis=-1).astype(BF16)
        gated = jnp.dot(inputs, wg[...], preferred_element_type=F32)
        upward = jnp.dot(inputs, wu[...], preferred_element_type=F32)
        act = (gated / (1.0 + jnp.exp(-gated)) * upward).astype(BF16)
        table = gate_grid[side].reshape(blocks * tok, 128)
        lanes = lax.broadcasted_iota(jnp.int32, table.shape, 1)
        return act, jnp.sum(jnp.where(lanes == expert, table, 0.0), axis=-1, keepdims=True)

    def down_a(side, act, scale):
        result = jnp.dot(act, wd[:, :half], preferred_element_type=F32) * scale
        packed = pack_rows(result.reshape(blocks, tok, half))
        res_a[side] = packed.reshape(2, 2, NZ, 2 * tok, half // 2)

    def down_b(side, act, scale):
        result = jnp.dot(act, wd[:, half:], preferred_element_type=F32) * scale
        packed = pack_rows(result.reshape(blocks, tok, half))
        for i in range(2):
            for j in range(2):
                first = (i * 2 + j) * NZ
                res_b[side, j, i] = packed[first : first + NZ]

    core_a.wait_recv()
    core_b.wait_recv()
    act, scale = activity(1 - c)
    down_a(1 - c, act, scale)
    rcore_a = send(res_a.at[1 - c], rc_a, ra_ss.at[0], ra_rs.at[0], peer_c)
    down_b(1 - c, act, scale)
    rcore_b = send(res_b.at[1 - c], rc_b, rb_ss.at[0], rb_rs.at[0], peer_c)
    act, scale = activity(c)
    down_a(c, act, scale)
    down_b(c, act, scale)

    def added(first, second):
        return (first.astype(F32) + second.astype(F32)).astype(BF16)

    rcore_a.wait_recv()
    s1_a[...] = added(res_a[c], rc_a[...])
    rone_a = send(s1_a.at[1 - x], r1_a, ra_ss.at[1], ra_rs.at[1], peer_x)
    rcore_b.wait_recv()
    s1_b[...] = added(res_b[c], rc_b[...])
    rone_b = send(s1_b.at[1 - y], r1_b, rb_ss.at[1], rb_rs.at[1], peer_y)
    rone_b.wait_recv()
    s2_b[...] = added(s1_b[y], r1_b[...])
    rone_a.wait_recv()
    s2_a[...] = added(s1_a[x], r1_a[...])
    rtwo_a = send(s2_a.at[1 - y], r2_a, ra_ss.at[2], ra_rs.at[2], peer_y)
    rtwo_b = send(s2_b.at[1 - x], r2_b, rb_ss.at[2], rb_rs.at[2], peer_x)
    rtwo_a.wait_recv()
    s3_a[...] = added(s2_a[y], r2_a[...])
    rz_a = [
        send(s3_a.at[(z + k) % NZ], r3_a.at[k], ra_ss.at[2 + k], ra_rs.at[2 + k], to_z(k))
        for k in range(1, NZ)
    ]
    rtwo_b.wait_recv()
    s3_b[...] = added(s2_b[x], r2_b[...])
    rz_b = [
        send(s3_b.at[(z + k) % NZ], r3_b.at[k], rb_ss.at[2 + k], rb_rs.at[2 + k], to_z(k))
        for k in range(1, NZ)
    ]
    sum_a = s3_a[z].astype(F32)
    sum_b = s3_b[z].astype(F32)
    for k in range(1, NZ):
        rz_a[k - 1].wait_recv()
        sum_a = sum_a + r3_a[k].astype(F32)
    for k in range(1, NZ):
        rz_b[k - 1].wait_recv()
        sum_b = sum_b + r3_b[k].astype(F32)
    moe = jnp.concatenate([sum_a[:tok], sum_a[tok:], sum_b[:tok], sum_b[tok:]], axis=-1)
    out_ref[...] = (mixed + moe).astype(BF16)
    for copy in started:
        copy.wait_send()


def local_kernel(
    tokens, attn_gain, w_qkv, q_gain, k_gain, w_out, prefix_keys, prefix_values, segments,
    request_group, prefix_owner, mlp_gain, expert_ids, gate_weights, w_gate, w_up, w_down,
):
    S, T = lax.axis_size("seq"), lax.axis_size("tensor")
    NZ = T // 2
    tok, width = tokens.shape
    cols = w_qkv.shape[2]
    tok_seq = tok * T
    slots = prefix_keys.shape[1]
    units = w_gate.shape[2]
    vm, dma = pltpu.VMEM, pltpu.SemaphoreType.DMA
    quarter = width // 4
    blk = (2 * tok, quarter)
    grid = vm((2, 2, 2, NZ) + blk, BF16)
    pair = lambda *lead: [vm(lead + blk, BF16)] * 2
    scratch = [
        vm((3, width, cols), BF16), vm((cols, width), BF16),
        vm((slots, cols), BF16), vm((slots, cols), BF16),
        vm((width, units), BF16), vm((width, units), BF16), vm((units, width), BF16),
        vm((T, 2 * tok, width // 2), BF16), vm((T, 8, 2 * tok_seq), F32),
        vm((S, 8, 2 * tok_seq), F32), vm((S, 2 * tok_seq, cols), BF16),
        *[vm((S, tok_seq, cols), BF16)] * 3,
        vm((T, 2 * tok, width // 2), BF16), vm((T, 2 * tok, width // 2), BF16),
        grid, grid, vm((2, 2, 2, NZ, tok, 128), F32),
        grid, grid,
        *pair(2, 2, NZ), *pair(2, 2, NZ), *pair(2, NZ),
        *pair(2, NZ), *pair(NZ), *pair(NZ), *pair(NZ),
        dma((7,)),
        *[dma((T,))] * 4, *[dma((S,))] * 8, *[dma((T,))] * 2,
        *[dma((8,))] * 10,
    ]
    in_vmem = pl.BlockSpec(memory_space=pltpu.VMEM)
    in_smem = pl.BlockSpec(memory_space=pltpu.SMEM)
    in_any = pl.BlockSpec(memory_space=pl.ANY)
    results = pl.pallas_call(
        functools.partial(layer_kernel, (S, T, NZ, EXP_DEV)),
        out_shape=(
            jax.ShapeDtypeStruct((tok, width), BF16),
            jax.ShapeDtypeStruct((tok_seq, cols), BF16),
            jax.ShapeDtypeStruct((tok_seq, cols), BF16),
        ),
        in_specs=[in_vmem] * 6 + [in_smem] * 2 + [in_vmem] * 2 + [in_any] * 7,
        out_specs=(in_vmem,) * 3,
        scratch_shapes=scratch,
        compiler_params=pltpu.CompilerParams(
            collective_id=0, has_side_effects=True, vmem_limit_bytes=56 * 2**20
        ),
    )(
        tokens, attn_gain, q_gain, k_gain, mlp_gain,
        segments[None], request_group, prefix_owner, expert_ids, gate_weights,
        jnp.transpose(w_qkv, (1, 0, 2)), w_out, prefix_keys, prefix_values, w_gate, w_up, w_down,
    )
    return pl.pallas_call(
        hand_on,
        out_shape=tuple(jax.ShapeDtypeStruct(r.shape, r.dtype) for r in results),
        in_specs=[in_vmem] * 3,
        out_specs=(in_vmem,) * 3,
    )(*results)


def hand_on(*refs):
    for source, target in zip(refs[:3], refs[3:]):
        target[...] = source[...]


def whole_heads(*arrays):
    seq_size, tensor_size = lax.axis_size("seq"), lax.axis_size("tensor")
    if arrays[2].shape[2] % HD == 0 and seq_size == 4 and tensor_size == 8:
        return local_kernel(*arrays)
    return local(*arrays)


def solution(mesh):
    return jax.shard_map(
        whole_heads,
        mesh=mesh,
        in_specs=(
            P(("seq", "tensor"), None),
            P(),
            P(None, None, "tensor"),
            P("tensor"),
            P("tensor"),
            P("tensor", None),
            P("seq", None, "tensor"),
            P("seq", None, "tensor"),
            P(),
            P(),
            P(),
            P(),
            P(("seq", "tensor"), None),
            P(("seq", "tensor"), None),
            P(("tensor", "seq"), None, None),
            P(("tensor", "seq"), None, None),
            P(("tensor", "seq"), None, None),
        ),
        out_specs=(P(("seq", "tensor"), None), P("seq", "tensor"), P("seq", "tensor")),
        check_vma=False,
    )
```

```python
import functools

import jax
import jax.numpy as jnp
from jax import lax
from jax.experimental import pallas as pl
from jax.experimental.pallas import tpu as pltpu
from jax.sharding import PartitionSpec as P

HD = 128
TOP = 8
EXP_DEV = 2


def from_partner(value, axis, stride):
    mask = 2**stride
    pairs = [(source, source ^ mask) for source in range(lax.axis_size(axis))]
    return lax.ppermute(value, axis, pairs)


def passed_along(value, axis, by):
    devices = lax.axis_size(axis)
    pairs = [(i, i + by) for i in range(devices) if 0 <= i + by < devices]
    return lax.ppermute(value, axis, pairs)


def rms_scale(values, gain):
    mean_square = jnp.mean(values * values, axis=-1, keepdims=True)
    return values * lax.rsqrt(mean_square + 1e-05) * gain.astype(jnp.float32)


def attend_block(carry, queries_heads, block, mask):
    largest, total, accum = carry
    heads_local = queries_heads.shape[1]
    count = block.shape[0]
    key_block = block[:, 0].reshape(count, heads_local, HD)
    value_block = block[:, 1].reshape(count, heads_local, HD)
    scores = jnp.einsum(
        "qhd,khd->hqk", queries_heads, key_block, preferred_element_type=jnp.float32
    ) * HD ** (-0.5)
    scores = jnp.where(mask[None], scores, -1e30)
    new_largest = jnp.maximum(largest, jnp.max(scores, axis=-1))
    weights = jnp.where(mask[None], jnp.exp(scores - new_largest[:, :, None]), 0.0)
    factor = jnp.exp(largest - new_largest)
    total = total * factor + jnp.sum(weights, axis=-1)
    update = jnp.einsum(
        "hqk,khd->hqd",
        weights.astype(jnp.bfloat16),
        value_block,
        preferred_element_type=jnp.float32,
    )
    accum = accum * factor[:, :, None] + update
    return (new_largest, total, accum)


def local(
    tokens,
    attn_gain,
    w_qkv,
    q_gain,
    k_gain,
    w_out,
    prefix_keys,
    prefix_values,
    segments,
    request_group,
    prefix_owner,
    mlp_gain,
    expert_ids,
    gate_weights,
    w_gate,
    w_up,
    w_down,
):
    tensor_size = lax.axis_size("tensor")
    seq_size = lax.axis_size("seq")
    seq_index = lax.axis_index("seq")
    tensor_index = lax.axis_index("tensor")
    tok_dev = tokens.shape[0]
    width = tokens.shape[1]
    tok_seq = tok_dev * tensor_size
    columns = w_qkv.shape[2]
    paired = columns < HD
    normed = rms_scale(tokens.astype(jnp.float32), attn_gain).astype(jnp.bfloat16)
    w_flat = w_qkv.reshape(width, 3 * columns)
    projected = jnp.dot(
        lax.all_gather(normed, "tensor", axis=0, tiled=True),
        w_flat,
        preferred_element_type=jnp.float32,
    )
    query_part = projected[:, :columns]
    key_part = projected[:, columns : 2 * columns]
    squares = lax.psum(
        (jnp.sum(query_part * query_part, axis=-1), jnp.sum(key_part * key_part, axis=-1)), "tensor"
    )
    query_rows = (
        query_part * lax.rsqrt(squares[0] / width + 1e-05)[:, None] * q_gain.astype(jnp.float32)
    ).astype(jnp.bfloat16)
    new_keys = (
        key_part * lax.rsqrt(squares[1] / width + 1e-05)[:, None] * k_gain.astype(jnp.float32)
    ).astype(jnp.bfloat16)
    new_values = projected[:, 2 * columns :].astype(jnp.bfloat16)
    stacked = jnp.stack(
        [
            jnp.concatenate([new_keys, prefix_keys[0]], axis=0),
            jnp.concatenate([new_values, prefix_values[0]], axis=0),
        ],
        axis=1,
    )
    half_rows = tok_seq // 2
    if paired:
        lower_bit = tensor_index % 2
        partner = from_partner(stacked, "tensor", 0)
        full = jnp.where(
            lower_bit == 0,
            jnp.concatenate([stacked, partner], axis=-1),
            jnp.concatenate([partner, stacked], axis=-1),
        )
        query_halves = query_rows.reshape(2, half_rows, columns)
        own_half = lax.dynamic_index_in_dim(query_halves, lower_bit, 0, keepdims=False)
        send_half = lax.dynamic_index_in_dim(query_halves, 1 - lower_bit, 0, keepdims=False)
        got_half = from_partner(send_half, "tensor", 0)
        query_full = jnp.where(
            lower_bit == 0,
            jnp.concatenate([own_half, got_half], axis=-1),
            jnp.concatenate([got_half, own_half], axis=-1),
        )
        query_count = half_rows
        query_offset = lower_bit * half_rows
        heads_local = 1
    else:
        full = stacked
        query_full = query_rows
        query_count = tok_seq
        query_offset = jnp.int32(0)
        heads_local = columns // HD
    suffix_full = full[:tok_seq]
    prefix_full = full[tok_seq:]
    queries_heads = query_full.reshape(query_count, heads_local, HD)
    groups_count = prefix_owner.shape[0]
    request_count = request_group.shape[0]
    token_group = jnp.sum(
        jnp.where(
            segments[:, None] == jnp.arange(request_count, dtype=jnp.int32)[None, :],
            request_group[None, :],
            0,
        ),
        axis=1,
    )
    base_row = seq_index * tok_seq
    query_start = base_row + query_offset
    query_seg = lax.dynamic_slice_in_dim(segments, query_start, query_count, 0)
    query_group = lax.dynamic_slice_in_dim(token_group, query_start, query_count, 0)
    query_pos = query_start + jnp.arange(query_count, dtype=jnp.int32)
    padded_seg = jnp.concatenate([jnp.full((tok_seq,), -1, jnp.int32), segments], axis=0)
    key_seg = lax.dynamic_slice_in_dim(padded_seg, base_row, 2 * tok_seq, 0)
    key_pos = base_row - tok_seq + jnp.arange(2 * tok_seq, dtype=jnp.int32)
    previous = passed_along(suffix_full, "seq", 1)
    suffix_keys = jnp.concatenate([previous, suffix_full], axis=0)
    suffix_mask = (key_seg[None, :] == query_seg[:, None]) & (
        key_pos[None, :] <= query_pos[:, None]
    )
    carry = (
        jnp.full((heads_local, query_count), -1e30, jnp.float32),
        jnp.zeros((heads_local, query_count), jnp.float32),
        jnp.zeros((heads_local, query_count, HD), jnp.float32),
    )
    carry = attend_block(carry, queries_heads, suffix_keys, suffix_mask)
    owner_of_query = jnp.sum(
        jnp.where(
            query_group[:, None] == jnp.arange(groups_count, dtype=jnp.int32)[None, :],
            prefix_owner[None, :],
            0,
        ),
        axis=1,
    )
    state = carry
    piece = lax.all_gather(prefix_full[None], "seq", axis=0, tiled=True)
    start = jnp.int32(0)
    for offset in range(piece.shape[0]):
        slot_mask = (owner_of_query == start + offset)[:, None]
        state = attend_block(state, queries_heads, piece[offset], slot_mask)
    carry = state
    attended = (carry[2] / carry[1][:, :, None]).astype(jnp.bfloat16)
    attended = jnp.transpose(attended, (1, 0, 2)).reshape(query_count, heads_local * HD)
    if paired:
        split_out = attended.reshape(query_count, 2, columns)
        own_out = lax.dynamic_index_in_dim(split_out, lower_bit, 1, keepdims=False)
        send_out = lax.dynamic_index_in_dim(split_out, 1 - lower_bit, 1, keepdims=False)
        got_out = from_partner(send_out, "tensor", 0)
        attended_local = jnp.where(
            lower_bit == 0,
            jnp.concatenate([own_out, got_out], axis=0),
            jnp.concatenate([got_out, own_out], axis=0),
        )
    else:
        attended_local = attended
    attn_sum = lax.psum_scatter(
        jnp.dot(attended_local, w_out, preferred_element_type=jnp.float32).astype(jnp.bfloat16),
        "tensor",
        scatter_dimension=0,
        tiled=True,
    ).astype(jnp.float32)
    mixed_rows = (tokens.astype(jnp.float32) + attn_sum).astype(jnp.bfloat16)
    expert_in = rms_scale(mixed_rows.astype(jnp.float32), mlp_gain).astype(jnp.bfloat16)
    exp_local = EXP_DEV
    experts_all = exp_local * tensor_size
    own_expert = seq_index // (seq_size // exp_local)
    capacity = max(2, 2 * tok_dev * TOP // experts_all)
    flat_ids = expert_ids.reshape(-1)
    onehot = (flat_ids[:, None] == jnp.arange(experts_all, dtype=jnp.int32)[None, :]).astype(
        jnp.int32
    )
    before = jnp.cumsum(onehot, axis=0) - onehot
    slot = flat_ids * capacity + jnp.sum(before * onehot, axis=1)
    slot_match = (
        slot.reshape(tok_dev, TOP)[:, :, None]
        == jnp.arange(experts_all * capacity, dtype=jnp.int32)[None, None, :]
    )
    dispatch_table = jnp.transpose(jnp.any(slot_match, axis=1)).astype(jnp.bfloat16)
    combine_table = jnp.sum(jnp.where(slot_match, gate_weights[:, :, None], 0.0), axis=1)
    buffer = jnp.dot(dispatch_table, expert_in, preferred_element_type=jnp.float32).astype(
        jnp.bfloat16
    )
    buffer = buffer.reshape(tensor_size, exp_local, capacity, width)
    received = lax.all_to_all(buffer, "tensor", split_axis=0, concat_axis=0, tiled=True)
    gate_local = w_gate[0]
    up_local = w_up[0]
    down_local = w_down[0]
    keep_expert = (jnp.arange(exp_local, dtype=jnp.int32) == own_expert)[None, None, :, None, None]
    chosen = lax.dynamic_index_in_dim(
        lax.all_gather(received[None], "seq", axis=0, tiled=True), own_expert, 2, keepdims=False
    )
    gated = jnp.einsum("srcd,df->srcf", chosen, gate_local, preferred_element_type=jnp.float32)
    upward = jnp.einsum("srcd,df->srcf", chosen, up_local, preferred_element_type=jnp.float32)
    activity = (jax.nn.silu(gated) * upward).astype(jnp.bfloat16)
    result = jnp.einsum("srcf,fd->srcd", activity, down_local, preferred_element_type=jnp.float32)
    partials = jnp.where(keep_expert, result[:, :, None], 0.0)
    summed = lax.psum_scatter(
        partials.astype(jnp.bfloat16), "seq", scatter_dimension=0, tiled=True
    ).astype(jnp.float32)
    returned = lax.all_to_all(
        summed[0].astype(jnp.bfloat16), "tensor", split_axis=0, concat_axis=0, tiled=True
    ).astype(jnp.float32)
    moe_sum = jnp.dot(
        combine_table,
        returned.reshape(experts_all * capacity, width),
        preferred_element_type=jnp.float32,
        precision=lax.Precision.HIGHEST,
    )
    output = (mixed_rows.astype(jnp.float32) + moe_sum).astype(jnp.bfloat16)
    return (output, new_keys, new_values)


MESH = pl.DeviceIdType.MESH
F32 = jnp.float32
BF16 = jnp.bfloat16


def pack_rows(value):
    half = value.shape[-1] // 2
    return jnp.concatenate([value[:, :, :half], value[:, :, half:]], axis=1).astype(BF16)


def unpack_rows(value):
    count, rows, half = value.shape
    wide = value.astype(F32).reshape(count, 2, rows // 2, half)
    left = wide[:, 0].reshape(count * (rows // 2), half)
    right = wide[:, 1].reshape(count * (rows // 2), half)
    return jnp.concatenate([left, right], axis=-1)


def layer_kernel(
    dims,
    tokens_ref, attn_gain_ref, q_gain_ref, k_gain_ref, mlp_gain_ref,
    seg_row_ref, request_ref, slot_ref, ids_ref, gates_ref,
    wqkv_hbm, wout_hbm, pk_hbm, pv_hbm, wg_hbm, wu_hbm, wd_hbm,
    out_ref, keys_ref, values_ref,
    wqkv, wout, pk, pv, wg, wu, wd,
    ag, sq, sums_grid, qv, ks, att_snd, att_in, rs_snd, rs_in,
    grid_a, grid_b, gate_grid,
    res_a, res_b, rc_a, rc_b, s1_a, s1_b, r1_a, r1_b,
    s2_a, s2_b, r2_a, r2_b, s3_a, s3_b, r3_a, r3_b,
    w_sem,
    ag_ss, ag_rs, sq_ss, sq_rs, qv_ss, qv_rs, ks_ss, ks_rs, sm_ss, sm_rs, att_ss, att_rs, rs_ss, rs_rs,
    gg_ss, gg_rs, ga_ss, ga_rs, gb_ss, gb_rs, ra_ss, ra_rs, rb_ss, rb_rs,
):
    S, T, NZ, exp_local = dims
    s = lax.axis_index("seq")
    t = lax.axis_index("tensor")
    x, c = s // 2, s % 2
    z, y = t // 2, t % 2
    tok, width = tokens_ref.shape
    cols = keys_ref.shape[1]
    tok_seq = tok * T
    total_tok = tok_seq * S
    started = []

    loads = [
        pltpu.make_async_copy(wqkv_hbm, wqkv, w_sem.at[0]),
        pltpu.make_async_copy(pk_hbm.at[0], pk, w_sem.at[1]),
        pltpu.make_async_copy(pv_hbm.at[0], pv, w_sem.at[2]),
        pltpu.make_async_copy(wout_hbm, wout, w_sem.at[3]),
        pltpu.make_async_copy(wg_hbm.at[0], wg, w_sem.at[4]),
        pltpu.make_async_copy(wu_hbm.at[0], wu, w_sem.at[5]),
        pltpu.make_async_copy(wd_hbm.at[0], wd, w_sem.at[6]),
    ]
    for load in loads:
        load.start()

    barrier = pltpu.get_barrier_semaphore()
    for k in range(1, T):
        pl.semaphore_signal(barrier, inc=1, device_id=(s, (t + k) % T), device_id_type=MESH)
    for k in range(1, S):
        pl.semaphore_signal(barrier, inc=1, device_id=((s + k) % S, t), device_id_type=MESH)

    def send(src, dst, send_sem, recv_sem, to):
        copy = pltpu.make_async_remote_copy(
            src_ref=src, dst_ref=dst, send_sem=send_sem, recv_sem=recv_sem,
            device_id=to, device_id_type=MESH,
        )
        copy.start()
        started.append(copy)
        return copy

    def to_tensor(k):
        return (s, (t + k) % T)

    def seq_peer(d):
        return ((x + d // 2) % 2) * 2 + (c + d % 2) % 2

    def to_seq(d):
        return (seq_peer(d), t)

    peer_x = ((1 - x) * 2 + c, t)
    peer_c = (x * 2 + 1 - c, t)
    peer_y = (s, z * 2 + 1 - y)

    def to_z(k):
        return (s, ((z + k) % NZ) * 2 + y)

    def rms(value, gain):
        mean_square = jnp.mean(value * value, axis=-1, keepdims=True)
        return value * lax.rsqrt(mean_square + 1e-05) * gain

    tokens = tokens_ref[...].astype(F32)
    normed = rms(tokens, attn_gain_ref[...].astype(F32).reshape(1, width))
    ag[t] = pack_rows(normed[None])[0]
    lane = lax.broadcasted_iota(jnp.int32, (tok, 128), 1)
    dense = jnp.zeros((tok, 128), F32)
    for k in range(ids_ref.shape[1]):
        dense = dense + jnp.where(ids_ref[:, k : k + 1] == lane, gates_ref[:, k : k + 1], 0.0)
    gate_grid[c, x, y, z] = dense
    pl.semaphore_wait(barrier, T + S - 2)
    ag_copies = [
        send(ag.at[t], ag.at[t], ag_ss.at[k], ag_rs.at[k], to_tensor(k)) for k in range(1, T)
    ]
    gg_z = [
        send(gate_grid.at[c, x, y, z], gate_grid.at[c, x, y, z], gg_ss.at[k], gg_rs.at[k], to_z(k))
        for k in range(1, NZ)
    ]
    for copy in ag_copies:
        copy.wait_recv()
    rows = unpack_rows(ag[...]).astype(BF16)
    loads[0].wait()
    proj_q = jnp.dot(rows, wqkv[0], preferred_element_type=F32)
    proj_k = jnp.dot(rows, wqkv[1], preferred_element_type=F32)

    ones = jnp.ones((8, cols), F32)
    nt = (((1,), (1,)), ((), ()))
    squares = jnp.concatenate([proj_q * proj_q, proj_k * proj_k], axis=0)
    sq[t] = lax.dot_general(
        ones, squares, nt, precision=lax.Precision.HIGHEST, preferred_element_type=F32
    )
    sq_copies = [
        send(sq.at[t], sq.at[t], sq_ss.at[k], sq_rs.at[k], to_tensor(k)) for k in range(1, T)
    ]
    for copy in gg_z:
        copy.wait_recv()
    gg_y = send(gate_grid.at[c, x, y], gate_grid.at[c, x, y], gg_ss.at[4], gg_rs.at[4], peer_y)
    proj_v = jnp.dot(rows, wqkv[2], preferred_element_type=F32).astype(BF16)
    values_ref[...] = proj_v
    qv[s, :tok_seq] = (proj_q * q_gain_ref[...].astype(F32).reshape(1, cols)).astype(BF16)
    qv[s, tok_seq:] = proj_v
    qv_copies = [send(qv.at[s], qv.at[s], qv_ss.at[k], qv_rs.at[k], to_seq(k)) for k in range(1, S)]
    for copy in sq_copies:
        copy.wait_recv()
    sums_row = sq[0]
    for k in range(1, T):
        sums_row = sums_row + sq[k]
    sums_grid[s] = sums_row
    sums_copies = [
        send(sums_grid.at[s], sums_grid.at[s], sm_ss.at[k], sm_rs.at[k], to_seq(k))
        for k in range(1, S)
    ]

    def inverse_columns(sums):
        turned = lax.dot_general(
            sums, jnp.full((8, 128), 0.125, F32), (((0,), (0,)), ((), ())),
            precision=lax.Precision.HIGHEST, preferred_element_type=F32,
        )
        return lax.rsqrt(turned / width + 1e-05)[:, :1]

    new_k = (
        proj_k * inverse_columns(sums_row)[tok_seq:] * k_gain_ref[...].astype(F32).reshape(1, cols)
    ).astype(BF16)
    keys_ref[...] = new_k
    ks[s] = new_k
    ks_copies = [send(ks.at[s], ks.at[s], ks_ss.at[k], ks_rs.at[k], to_seq(k)) for k in range(1, S)]
    gg_y.wait_recv()
    gg_x = send(gate_grid.at[c, x], gate_grid.at[c, x], gg_ss.at[5], gg_rs.at[5], peer_x)
    seg_row = seg_row_ref[...]
    owner_row = jnp.zeros(seg_row.shape, jnp.int32)
    for r in range(request_ref.shape[0]):
        slot = jnp.int32(0)
        for g in range(slot_ref.shape[0]):
            slot = jnp.where(request_ref[r] == g, slot_ref[g], slot)
        owner_row = jnp.where(seg_row == r, slot, owner_row)
    chip_tok = 2 * tok_seq
    own_chip, next_chip = x, 1 - x

    def masks(chip):
        pos_q = lax.broadcasted_iota(jnp.int32, (chip_tok, total_tok), 0) + chip * chip_tok
        pos_k = lax.broadcasted_iota(jnp.int32, (chip_tok, total_tok), 1)

        def as_column(row):
            wide = jnp.where(pos_q == pos_k, row.astype(F32), 0.0)
            return jnp.sum(wide, axis=-1, keepdims=True).astype(jnp.int32)

        mask = (as_column(seg_row) == seg_row) & (pos_k <= pos_q)
        return mask, as_column(owner_row) == s

    def queries_of(chip):
        rows = qv[pl.ds(2 * chip, 2), :tok_seq].reshape(chip_tok, cols)
        sums = sums_grid[pl.ds(2 * chip, 2)]
        scale = jnp.concatenate([inverse_columns(sums[k])[:tok_seq] for k in range(2)], axis=0)
        return rows, scale * HD ** (-0.5)

    def prefix_part(rows, scale):
        parts = []
        for h in range(cols // HD):
            part = slice(h * HD, (h + 1) * HD)
            pre = lax.dot_general(rows[:, part], pk[:, part], nt, preferred_element_type=F32)
            pre = pre * scale
            top = jnp.max(pre, axis=-1, keepdims=True)
            pre = jnp.exp(pre - top)
            total = jnp.sum(pre, axis=-1, keepdims=True)
            mix = jnp.dot(pre.astype(BF16), pv[:, part], preferred_element_type=F32)
            parts.append((top, total, mix))
        return parts

    def with_suffix(chip, rows, scale, parts, mask, mine):
        all_v = qv[:, tok_seq:].reshape(total_tok, cols)
        all_k = ks[...].reshape(total_tok, cols)
        heads = []
        for h in range(cols // HD):
            part = slice(h * HD, (h + 1) * HD)
            top_p, total_p, mix_p = parts[h]
            suf = lax.dot_general(rows[:, part], all_k[:, part], nt, preferred_element_type=F32)
            suf = jnp.where(mask, suf * scale, -1e30)
            top = jnp.maximum(top_p, jnp.max(suf, axis=-1, keepdims=True))
            suf = jnp.where(mask, jnp.exp(suf - top), 0.0)
            factor = jnp.exp(top_p - top)
            total = total_p * factor + jnp.sum(suf, axis=-1, keepdims=True)
            mix = jnp.dot(suf.astype(BF16), all_v[:, part], preferred_element_type=F32)
            mix = mix_p * factor + mix
            heads.append(jnp.where(mine, mix / total, 0.0).astype(BF16))
        out = jnp.concatenate(heads, axis=-1).reshape(2, tok_seq, cols)
        att_snd[pl.ds(2 * chip, 2)] = out

    mask_own, mine_own = masks(own_chip)
    mask_next, mine_next = masks(next_chip)
    loads[1].wait()
    loads[2].wait()
    qv_copies[0].wait_recv()
    sums_copies[0].wait_recv()
    rows_own, scale_own = queries_of(own_chip)
    parts_own = prefix_part(rows_own, scale_own)
    for copy in qv_copies[1:] + sums_copies[1:]:
        copy.wait_recv()
    rows_next, scale_next = queries_of(next_chip)
    parts_next = prefix_part(rows_next, scale_next)
    for copy in ks_copies:
        copy.wait_recv()

    def send_attended(d):
        return send(att_snd.at[seq_peer(d)], att_in.at[d], att_ss.at[d], att_rs.at[d], to_seq(d))

    with_suffix(next_chip, rows_next, scale_next, parts_next, mask_next, mine_next)
    far_copies = [send_attended(2), send_attended(3)]
    with_suffix(own_chip, rows_own, scale_own, parts_own, mask_own, mine_own)
    att_copies = [send_attended(1)] + far_copies
    gg_x.wait_recv()
    gg_c = send(gate_grid.at[c], gate_grid.at[c], gg_ss.at[6], gg_rs.at[6], peer_c)
    attended = att_snd[s].astype(F32)
    for k in range(1, S):
        att_copies[k - 1].wait_recv()
        attended = attended + att_in[k].astype(F32)
    loads[3].wait()
    partial = jnp.dot(attended.astype(BF16), wout[...], preferred_element_type=F32)
    rs_snd[...] = pack_rows(partial.reshape(T, tok, width))
    rs_copies = [
        send(rs_snd.at[(t + k) % T], rs_in.at[k], rs_ss.at[k], rs_rs.at[k], to_tensor(k))
        for k in range(1, T)
    ]
    attn_sum = rs_snd[t].astype(F32)
    for k in range(1, T):
        rs_copies[k - 1].wait_recv()
        attn_sum = attn_sum + rs_in[k].astype(F32)
    attn_sum = jnp.concatenate([attn_sum[:tok], attn_sum[tok:]], axis=-1)
    mixed = (tokens + attn_sum).astype(BF16).astype(F32)
    expert_in = rms(mixed, mlp_gain_ref[...].astype(F32).reshape(1, width))

    half = width // 2
    grid_a[c, x, y, z] = pack_rows(expert_in[None, :, :half])[0]
    grid_b[c, y, x, z] = pack_rows(expert_in[None, :, half:])[0]
    mine_a, mine_b = grid_a.at[c, x, y, z], grid_b.at[c, y, x, z]

    def z_stage(own, ss, rs):
        return [send(own, own, ss.at[k], rs.at[k], to_z(k)) for k in range(1, NZ)]

    def hand_block(grid, i, j, k, ss, rs, to):
        block = grid.at[c, i, j, (z - k + NZ) % NZ]
        return send(block, block, ss.at[4 + k], rs.at[4 + k], to)

    z_a = z_stage(mine_a, ga_ss, ga_rs)
    z_b = z_stage(mine_b, gb_ss, gb_rs)
    two_a = [hand_block(grid_a, x, y, 0, ga_ss, ga_rs, peer_y)]
    two_b = [hand_block(grid_b, y, x, 0, gb_ss, gb_rs, peer_x)]
    for k in (1, NZ - 1, *range(2, NZ - 1)):
        z_a[k - 1].wait_recv()
        two_a.append(hand_block(grid_a, x, y, k, ga_ss, ga_rs, peer_y))
        z_b[k - 1].wait_recv()
        two_b.append(hand_block(grid_b, y, x, k, gb_ss, gb_rs, peer_x))

    def hand_row(grid, i, j, n, ss, rs, to):
        row = grid.at[c, i, j]
        return send(row, row, ss.at[n], rs.at[n], to)

    one_a = [hand_row(grid_a, x, y, 8, ga_ss, ga_rs, peer_x)]
    one_b = [hand_row(grid_b, y, x, 8, gb_ss, gb_rs, peer_y)]
    for copy in two_a:
        copy.wait_recv()
    one_a.append(hand_row(grid_a, x, 1 - y, 9, ga_ss, ga_rs, peer_x))
    core_a = [send(grid_a.at[c, x], grid_a.at[c, x], ga_ss.at[10], ga_rs.at[10], peer_c)]
    for copy in two_b:
        copy.wait_recv()
    one_b.append(hand_row(grid_b, y, 1 - x, 9, gb_ss, gb_rs, peer_y))
    core_b = [send(grid_b.at[c, y], grid_b.at[c, y], gb_ss.at[10], gb_rs.at[10], peer_c)]
    for copy in one_a:
        copy.wait_recv()
    core_a.append(send(grid_a.at[c, 1 - x], grid_a.at[c, 1 - x], ga_ss.at[11], ga_rs.at[11], peer_c))
    for copy in one_b:
        copy.wait_recv()
    core_b.append(send(grid_b.at[c, 1 - y], grid_b.at[c, 1 - y], gb_ss.at[11], gb_rs.at[11], peer_c))
    for load in loads[4:]:
        load.wait()
    gg_c.wait_recv()
    expert = exp_local * t + s // (S // exp_local)
    blocks = 4 * NZ

    def activity(side):
        block_a = grid_a[side].reshape(blocks, 2 * tok, half // 2)
        raw_b = grid_b[side]
        block_b = jnp.concatenate([raw_b[j, i] for i in range(2) for j in range(2)], axis=0)
        inputs = jnp.concatenate([unpack_rows(block_a), unpack_rows(block_b)], axis=-1).astype(BF16)
        gated = jnp.dot(inputs, wg[...], preferred_element_type=F32)
        upward = jnp.dot(inputs, wu[...], preferred_element_type=F32)
        act = (gated / (1.0 + jnp.exp(-gated)) * upward).astype(BF16)
        table = gate_grid[side].reshape(blocks * tok, 128)
        lanes = lax.broadcasted_iota(jnp.int32, table.shape, 1)
        return act, jnp.sum(jnp.where(lanes == expert, table, 0.0), axis=-1, keepdims=True)

    def down_a(side, act, scale):
        result = jnp.dot(act, wd[:, :half], preferred_element_type=F32) * scale
        packed = pack_rows(result.reshape(blocks, tok, half))
        res_a[side] = packed.reshape(2, 2, NZ, 2 * tok, half // 2)

    def down_b(side, act, scale):
        result = jnp.dot(act, wd[:, half:], preferred_element_type=F32) * scale
        packed = pack_rows(result.reshape(blocks, tok, half))
        for i in range(2):
            for j in range(2):
                first = (i * 2 + j) * NZ
                res_b[side, j, i] = packed[first : first + NZ]

    for copy in core_a + core_b:
        copy.wait_recv()
    act, scale = activity(1 - c)
    down_a(1 - c, act, scale)
    rcore_a = send(res_a.at[1 - c], rc_a, ra_ss.at[0], ra_rs.at[0], peer_c)
    down_b(1 - c, act, scale)
    rcore_b = send(res_b.at[1 - c], rc_b, rb_ss.at[0], rb_rs.at[0], peer_c)
    act, scale = activity(c)
    down_a(c, act, scale)
    down_b(c, act, scale)

    def added(first, second):
        return (first.astype(F32) + second.astype(F32)).astype(BF16)

    rcore_a.wait_recv()
    s1_a[...] = added(res_a[c], rc_a[...])

    def row_out(s1, r1, i, j, n, ss, rs, to):
        return send(s1.at[1 - i, j], r1.at[j], ss.at[n], rs.at[n], to)

    rone_a = [row_out(s1_a, r1_a, x, 1 - y, 1, ra_ss, ra_rs, peer_x)]
    rone_a.append(row_out(s1_a, r1_a, x, y, 2, ra_ss, ra_rs, peer_x))
    rcore_b.wait_recv()
    s1_b[...] = added(res_b[c], rc_b[...])
    rone_b = [row_out(s1_b, r1_b, y, 1 - x, 1, rb_ss, rb_rs, peer_y)]
    rone_b.append(row_out(s1_b, r1_b, y, x, 2, rb_ss, rb_rs, peer_y))
    rone_a[0].wait_recv()
    s2_a[1 - y] = added(s1_a[x, 1 - y], r1_a[1 - y])
    rtwo_a = send(s2_a.at[1 - y], r2_a, ra_ss.at[3], ra_rs.at[3], peer_y)
    rone_b[0].wait_recv()
    s2_b[1 - x] = added(s1_b[y, 1 - x], r1_b[1 - x])
    rtwo_b = send(s2_b.at[1 - x], r2_b, rb_ss.at[3], rb_rs.at[3], peer_x)
    rone_a[1].wait_recv()
    s2_a[y] = added(s1_a[x, y], r1_a[y])
    rone_b[1].wait_recv()
    s2_b[x] = added(s1_b[y, x], r1_b[x])

    def z_out(s3, r3, k, ss, rs):
        return send(s3.at[(z + k) % NZ], r3.at[k], ss.at[3 + k], rs.at[3 + k], to_z(k))

    rtwo_a.wait_recv()
    s3_a[...] = added(s2_a[y], r2_a[...])
    rz_a = [z_out(s3_a, r3_a, k, ra_ss, ra_rs) for k in range(1, NZ)]
    rtwo_b.wait_recv()
    s3_b[...] = added(s2_b[x], r2_b[...])
    rz_b = [z_out(s3_b, r3_b, k, rb_ss, rb_rs) for k in range(1, NZ)]
    sum_a = s3_a[z].astype(F32)
    sum_b = s3_b[z].astype(F32)
    for k in range(1, NZ):
        rz_a[k - 1].wait_recv()
        sum_a = sum_a + r3_a[k].astype(F32)
    for k in range(1, NZ):
        rz_b[k - 1].wait_recv()
        sum_b = sum_b + r3_b[k].astype(F32)
    moe = jnp.concatenate([sum_a[:tok], sum_a[tok:], sum_b[:tok], sum_b[tok:]], axis=-1)
    out_ref[...] = (mixed + moe).astype(BF16)
    for copy in started:
        copy.wait_send()


def local_kernel(
    tokens, attn_gain, w_qkv, q_gain, k_gain, w_out, prefix_keys, prefix_values, segments,
    request_group, prefix_owner, mlp_gain, expert_ids, gate_weights, w_gate, w_up, w_down,
):
    S, T = lax.axis_size("seq"), lax.axis_size("tensor")
    NZ = T // 2
    tok, width = tokens.shape
    cols = w_qkv.shape[2]
    tok_seq = tok * T
    slots = prefix_keys.shape[1]
    units = w_gate.shape[2]
    vm, dma = pltpu.VMEM, pltpu.SemaphoreType.DMA
    quarter = width // 4
    blk = (2 * tok, quarter)
    grid = vm((2, 2, 2, NZ) + blk, BF16)
    pair = lambda *lead: [vm(lead + blk, BF16)] * 2
    scratch = [
        vm((3, width, cols), BF16), vm((cols, width), BF16),
        vm((slots, cols), BF16), vm((slots, cols), BF16),
        vm((width, units), BF16), vm((width, units), BF16), vm((units, width), BF16),
        vm((T, 2 * tok, width // 2), BF16), vm((T, 8, 2 * tok_seq), F32),
        vm((S, 8, 2 * tok_seq), F32), vm((S, 2 * tok_seq, cols), BF16),
        *[vm((S, tok_seq, cols), BF16)] * 3,
        vm((T, 2 * tok, width // 2), BF16), vm((T, 2 * tok, width // 2), BF16),
        grid, grid, vm((2, 2, 2, NZ, tok, 128), F32),
        grid, grid,
        *pair(2, 2, NZ), *pair(2, 2, NZ), *pair(2, NZ),
        *pair(2, NZ), *pair(NZ), *pair(NZ), *pair(NZ),
        dma((7,)),
        *[dma((T,))] * 4, *[dma((S,))] * 8, *[dma((T,))] * 2,
        *[dma((8,))] * 2, *[dma((NZ + 8,))] * 8,
    ]
    in_vmem = pl.BlockSpec(memory_space=pltpu.VMEM)
    in_smem = pl.BlockSpec(memory_space=pltpu.SMEM)
    in_any = pl.BlockSpec(memory_space=pl.ANY)
    results = pl.pallas_call(
        functools.partial(layer_kernel, (S, T, NZ, EXP_DEV)),
        out_shape=(
            jax.ShapeDtypeStruct((tok, width), BF16),
            jax.ShapeDtypeStruct((tok_seq, cols), BF16),
            jax.ShapeDtypeStruct((tok_seq, cols), BF16),
        ),
        in_specs=[in_vmem] * 6 + [in_smem] * 2 + [in_vmem] * 2 + [in_any] * 7,
        out_specs=(in_vmem,) * 3,
        scratch_shapes=scratch,
        compiler_params=pltpu.CompilerParams(
            collective_id=0, has_side_effects=True, vmem_limit_bytes=56 * 2**20
        ),
    )(
        tokens, attn_gain, q_gain, k_gain, mlp_gain,
        segments[None], request_group, prefix_owner, expert_ids, gate_weights,
        jnp.transpose(w_qkv, (1, 0, 2)), w_out, prefix_keys, prefix_values, w_gate, w_up, w_down,
    )
    return pl.pallas_call(
        hand_on,
        out_shape=tuple(jax.ShapeDtypeStruct(r.shape, r.dtype) for r in results),
        in_specs=[in_vmem] * 3,
        out_specs=(in_vmem,) * 3,
    )(*results)


def hand_on(*refs):
    for source, target in zip(refs[:3], refs[3:]):
        target[...] = source[...]


def whole_heads(*arrays):
    seq_size, tensor_size = lax.axis_size("seq"), lax.axis_size("tensor")
    if arrays[2].shape[2] % HD == 0 and seq_size == 4 and tensor_size == 8:
        return local_kernel(*arrays)
    return local(*arrays)


def solution(mesh):
    return jax.shard_map(
        whole_heads,
        mesh=mesh,
        in_specs=(
            P(("seq", "tensor"), None),
            P(),
            P(None, None, "tensor"),
            P("tensor"),
            P("tensor"),
            P("tensor", None),
            P("seq", None, "tensor"),
            P("seq", None, "tensor"),
            P(),
            P(),
            P(),
            P(),
            P(("seq", "tensor"), None),
            P(("seq", "tensor"), None),
            P(("tensor", "seq"), None, None),
            P(("tensor", "seq"), None, None),
            P(("tensor", "seq"), None, None),
        ),
        out_specs=(P(("seq", "tensor"), None), P("seq", "tensor"), P("seq", "tensor")),
        check_vma=False,
    )
```

```python
import functools

import jax
import jax.numpy as jnp
from jax import lax
from jax.experimental import pallas as pl
from jax.experimental.pallas import tpu as pltpu
from jax.sharding import PartitionSpec as P

HD = 128
TOP = 8
EXP_DEV = 2


def from_partner(value, axis, stride):
    mask = 2**stride
    pairs = [(source, source ^ mask) for source in range(lax.axis_size(axis))]
    return lax.ppermute(value, axis, pairs)


def passed_along(value, axis, by):
    devices = lax.axis_size(axis)
    pairs = [(i, i + by) for i in range(devices) if 0 <= i + by < devices]
    return lax.ppermute(value, axis, pairs)


def rms_scale(values, gain):
    mean_square = jnp.mean(values * values, axis=-1, keepdims=True)
    return values * lax.rsqrt(mean_square + 1e-05) * gain.astype(jnp.float32)


def attend_block(carry, queries_heads, block, mask):
    largest, total, accum = carry
    heads_local = queries_heads.shape[1]
    count = block.shape[0]
    key_block = block[:, 0].reshape(count, heads_local, HD)
    value_block = block[:, 1].reshape(count, heads_local, HD)
    scores = jnp.einsum(
        "qhd,khd->hqk", queries_heads, key_block, preferred_element_type=jnp.float32
    ) * HD ** (-0.5)
    scores = jnp.where(mask[None], scores, -1e30)
    new_largest = jnp.maximum(largest, jnp.max(scores, axis=-1))
    weights = jnp.where(mask[None], jnp.exp(scores - new_largest[:, :, None]), 0.0)
    factor = jnp.exp(largest - new_largest)
    total = total * factor + jnp.sum(weights, axis=-1)
    update = jnp.einsum(
        "hqk,khd->hqd",
        weights.astype(jnp.bfloat16),
        value_block,
        preferred_element_type=jnp.float32,
    )
    accum = accum * factor[:, :, None] + update
    return (new_largest, total, accum)


def local(
    tokens,
    attn_gain,
    w_qkv,
    q_gain,
    k_gain,
    w_out,
    prefix_keys,
    prefix_values,
    segments,
    request_group,
    prefix_owner,
    mlp_gain,
    expert_ids,
    gate_weights,
    w_gate,
    w_up,
    w_down,
):
    tensor_size = lax.axis_size("tensor")
    seq_size = lax.axis_size("seq")
    seq_index = lax.axis_index("seq")
    tensor_index = lax.axis_index("tensor")
    tok_dev = tokens.shape[0]
    width = tokens.shape[1]
    tok_seq = tok_dev * tensor_size
    columns = w_qkv.shape[2]
    paired = columns < HD
    normed = rms_scale(tokens.astype(jnp.float32), attn_gain).astype(jnp.bfloat16)
    w_flat = w_qkv.reshape(width, 3 * columns)
    projected = jnp.dot(
        lax.all_gather(normed, "tensor", axis=0, tiled=True),
        w_flat,
        preferred_element_type=jnp.float32,
    )
    query_part = projected[:, :columns]
    key_part = projected[:, columns : 2 * columns]
    squares = lax.psum(
        (jnp.sum(query_part * query_part, axis=-1), jnp.sum(key_part * key_part, axis=-1)), "tensor"
    )
    query_rows = (
        query_part * lax.rsqrt(squares[0] / width + 1e-05)[:, None] * q_gain.astype(jnp.float32)
    ).astype(jnp.bfloat16)
    new_keys = (
        key_part * lax.rsqrt(squares[1] / width + 1e-05)[:, None] * k_gain.astype(jnp.float32)
    ).astype(jnp.bfloat16)
    new_values = projected[:, 2 * columns :].astype(jnp.bfloat16)
    stacked = jnp.stack(
        [
            jnp.concatenate([new_keys, prefix_keys[0]], axis=0),
            jnp.concatenate([new_values, prefix_values[0]], axis=0),
        ],
        axis=1,
    )
    half_rows = tok_seq // 2
    if paired:
        lower_bit = tensor_index % 2
        partner = from_partner(stacked, "tensor", 0)
        full = jnp.where(
            lower_bit == 0,
            jnp.concatenate([stacked, partner], axis=-1),
            jnp.concatenate([partner, stacked], axis=-1),
        )
        query_halves = query_rows.reshape(2, half_rows, columns)
        own_half = lax.dynamic_index_in_dim(query_halves, lower_bit, 0, keepdims=False)
        send_half = lax.dynamic_index_in_dim(query_halves, 1 - lower_bit, 0, keepdims=False)
        got_half = from_partner(send_half, "tensor", 0)
        query_full = jnp.where(
            lower_bit == 0,
            jnp.concatenate([own_half, got_half], axis=-1),
            jnp.concatenate([got_half, own_half], axis=-1),
        )
        query_count = half_rows
        query_offset = lower_bit * half_rows
        heads_local = 1
    else:
        full = stacked
        query_full = query_rows
        query_count = tok_seq
        query_offset = jnp.int32(0)
        heads_local = columns // HD
    suffix_full = full[:tok_seq]
    prefix_full = full[tok_seq:]
    queries_heads = query_full.reshape(query_count, heads_local, HD)
    groups_count = prefix_owner.shape[0]
    request_count = request_group.shape[0]
    token_group = jnp.sum(
        jnp.where(
            segments[:, None] == jnp.arange(request_count, dtype=jnp.int32)[None, :],
            request_group[None, :],
            0,
        ),
        axis=1,
    )
    base_row = seq_index * tok_seq
    query_start = base_row + query_offset
    query_seg = lax.dynamic_slice_in_dim(segments, query_start, query_count, 0)
    query_group = lax.dynamic_slice_in_dim(token_group, query_start, query_count, 0)
    query_pos = query_start + jnp.arange(query_count, dtype=jnp.int32)
    padded_seg = jnp.concatenate([jnp.full((tok_seq,), -1, jnp.int32), segments], axis=0)
    key_seg = lax.dynamic_slice_in_dim(padded_seg, base_row, 2 * tok_seq, 0)
    key_pos = base_row - tok_seq + jnp.arange(2 * tok_seq, dtype=jnp.int32)
    previous = passed_along(suffix_full, "seq", 1)
    suffix_keys = jnp.concatenate([previous, suffix_full], axis=0)
    suffix_mask = (key_seg[None, :] == query_seg[:, None]) & (
        key_pos[None, :] <= query_pos[:, None]
    )
    carry = (
        jnp.full((heads_local, query_count), -1e30, jnp.float32),
        jnp.zeros((heads_local, query_count), jnp.float32),
        jnp.zeros((heads_local, query_count, HD), jnp.float32),
    )
    carry = attend_block(carry, queries_heads, suffix_keys, suffix_mask)
    owner_of_query = jnp.sum(
        jnp.where(
            query_group[:, None] == jnp.arange(groups_count, dtype=jnp.int32)[None, :],
            prefix_owner[None, :],
            0,
        ),
        axis=1,
    )
    state = carry
    piece = lax.all_gather(prefix_full[None], "seq", axis=0, tiled=True)
    start = jnp.int32(0)
    for offset in range(piece.shape[0]):
        slot_mask = (owner_of_query == start + offset)[:, None]
        state = attend_block(state, queries_heads, piece[offset], slot_mask)
    carry = state
    attended = (carry[2] / carry[1][:, :, None]).astype(jnp.bfloat16)
    attended = jnp.transpose(attended, (1, 0, 2)).reshape(query_count, heads_local * HD)
    if paired:
        split_out = attended.reshape(query_count, 2, columns)
        own_out = lax.dynamic_index_in_dim(split_out, lower_bit, 1, keepdims=False)
        send_out = lax.dynamic_index_in_dim(split_out, 1 - lower_bit, 1, keepdims=False)
        got_out = from_partner(send_out, "tensor", 0)
        attended_local = jnp.where(
            lower_bit == 0,
            jnp.concatenate([own_out, got_out], axis=0),
            jnp.concatenate([got_out, own_out], axis=0),
        )
    else:
        attended_local = attended
    attn_sum = lax.psum_scatter(
        jnp.dot(attended_local, w_out, preferred_element_type=jnp.float32).astype(jnp.bfloat16),
        "tensor",
        scatter_dimension=0,
        tiled=True,
    ).astype(jnp.float32)
    mixed_rows = (tokens.astype(jnp.float32) + attn_sum).astype(jnp.bfloat16)
    expert_in = rms_scale(mixed_rows.astype(jnp.float32), mlp_gain).astype(jnp.bfloat16)
    exp_local = EXP_DEV
    experts_all = exp_local * tensor_size
    own_expert = seq_index // (seq_size // exp_local)
    capacity = max(2, 2 * tok_dev * TOP // experts_all)
    flat_ids = expert_ids.reshape(-1)
    onehot = (flat_ids[:, None] == jnp.arange(experts_all, dtype=jnp.int32)[None, :]).astype(
        jnp.int32
    )
    before = jnp.cumsum(onehot, axis=0) - onehot
    slot = flat_ids * capacity + jnp.sum(before * onehot, axis=1)
    slot_match = (
        slot.reshape(tok_dev, TOP)[:, :, None]
        == jnp.arange(experts_all * capacity, dtype=jnp.int32)[None, None, :]
    )
    dispatch_table = jnp.transpose(jnp.any(slot_match, axis=1)).astype(jnp.bfloat16)
    combine_table = jnp.sum(jnp.where(slot_match, gate_weights[:, :, None], 0.0), axis=1)
    buffer = jnp.dot(dispatch_table, expert_in, preferred_element_type=jnp.float32).astype(
        jnp.bfloat16
    )
    buffer = buffer.reshape(tensor_size, exp_local, capacity, width)
    received = lax.all_to_all(buffer, "tensor", split_axis=0, concat_axis=0, tiled=True)
    gate_local = w_gate[0]
    up_local = w_up[0]
    down_local = w_down[0]
    keep_expert = (jnp.arange(exp_local, dtype=jnp.int32) == own_expert)[None, None, :, None, None]
    chosen = lax.dynamic_index_in_dim(
        lax.all_gather(received[None], "seq", axis=0, tiled=True), own_expert, 2, keepdims=False
    )
    gated = jnp.einsum("srcd,df->srcf", chosen, gate_local, preferred_element_type=jnp.float32)
    upward = jnp.einsum("srcd,df->srcf", chosen, up_local, preferred_element_type=jnp.float32)
    activity = (jax.nn.silu(gated) * upward).astype(jnp.bfloat16)
    result = jnp.einsum("srcf,fd->srcd", activity, down_local, preferred_element_type=jnp.float32)
    partials = jnp.where(keep_expert, result[:, :, None], 0.0)
    summed = lax.psum_scatter(
        partials.astype(jnp.bfloat16), "seq", scatter_dimension=0, tiled=True
    ).astype(jnp.float32)
    returned = lax.all_to_all(
        summed[0].astype(jnp.bfloat16), "tensor", split_axis=0, concat_axis=0, tiled=True
    ).astype(jnp.float32)
    moe_sum = jnp.dot(
        combine_table,
        returned.reshape(experts_all * capacity, width),
        preferred_element_type=jnp.float32,
        precision=lax.Precision.HIGHEST,
    )
    output = (mixed_rows.astype(jnp.float32) + moe_sum).astype(jnp.bfloat16)
    return (output, new_keys, new_values)


MESH = pl.DeviceIdType.MESH
F32 = jnp.float32
BF16 = jnp.bfloat16


def pack_rows(value):
    half = value.shape[-1] // 2
    return jnp.concatenate([value[:, :, :half], value[:, :, half:]], axis=1).astype(BF16)


def unpack_rows(value):
    count, rows, half = value.shape
    wide = value.astype(F32).reshape(count, 2, rows // 2, half)
    left = wide[:, 0].reshape(count * (rows // 2), half)
    right = wide[:, 1].reshape(count * (rows // 2), half)
    return jnp.concatenate([left, right], axis=-1)


def layer_kernel(
    dims,
    tokens_ref, attn_gain_ref, q_gain_ref, k_gain_ref, mlp_gain_ref,
    seg_row_ref, request_ref, slot_ref, ids_ref, gates_ref,
    wqkv_hbm, wout_hbm, pk_hbm, pv_hbm, wg_hbm, wu_hbm, wd_hbm,
    out_ref, keys_ref, values_ref,
    wqkv, wout, pk, pv, wg, wu, wd,
    ag, sq, sums_grid, qv, ks, att_snd, att_in, rs_snd, rs_in,
    grid_a, grid_b, gate_grid,
    res_a, res_b, rc_a, rc_b, s1_a, s1_b, r1_a, r1_b,
    s2_a, s2_b, r2_a, r2_b, s3_a, s3_b, r3_a, r3_b,
    w_sem,
    ag_ss, ag_rs, sq_ss, sq_rs, qv_ss, qv_rs, ks_ss, ks_rs, sm_ss, sm_rs, att_ss, att_rs, rs_ss, rs_rs,
    gg_ss, gg_rs, ga_ss, ga_rs, gb_ss, gb_rs, ra_ss, ra_rs, rb_ss, rb_rs,
):
    S, T, NZ, exp_local = dims
    s = lax.axis_index("seq")
    t = lax.axis_index("tensor")
    x, c = s // 2, s % 2
    z, y = t // 2, t % 2
    tok, width = tokens_ref.shape
    cols = keys_ref.shape[1]
    tok_seq = tok * T
    total_tok = tok_seq * S
    started = []

    loads = [
        pltpu.make_async_copy(wqkv_hbm, wqkv, w_sem.at[0]),
        pltpu.make_async_copy(pk_hbm.at[0], pk, w_sem.at[1]),
        pltpu.make_async_copy(pv_hbm.at[0], pv, w_sem.at[2]),
        pltpu.make_async_copy(wout_hbm, wout, w_sem.at[3]),
        pltpu.make_async_copy(wg_hbm.at[0], wg, w_sem.at[4]),
        pltpu.make_async_copy(wu_hbm.at[0], wu, w_sem.at[5]),
        pltpu.make_async_copy(wd_hbm.at[0], wd, w_sem.at[6]),
    ]
    for load in loads:
        load.start()

    barrier = pltpu.get_barrier_semaphore()
    for k in range(1, T):
        pl.semaphore_signal(barrier, inc=1, device_id=(s, (t + k) % T), device_id_type=MESH)
    for k in range(1, S):
        pl.semaphore_signal(barrier, inc=1, device_id=((s + k) % S, t), device_id_type=MESH)

    def send(src, dst, send_sem, recv_sem, to):
        copy = pltpu.make_async_remote_copy(
            src_ref=src, dst_ref=dst, send_sem=send_sem, recv_sem=recv_sem,
            device_id=to, device_id_type=MESH,
        )
        copy.start()
        started.append(copy)
        return copy

    def to_tensor(k):
        return (s, (t + k) % T)

    def seq_peer(d):
        return ((x + d // 2) % 2) * 2 + (c + d % 2) % 2

    def to_seq(d):
        return (seq_peer(d), t)

    peer_x = ((1 - x) * 2 + c, t)
    peer_c = (x * 2 + 1 - c, t)
    peer_y = (s, z * 2 + 1 - y)

    def to_z(k):
        return (s, ((z + k) % NZ) * 2 + y)

    def rms(value, gain):
        mean_square = jnp.mean(value * value, axis=-1, keepdims=True)
        return value * lax.rsqrt(mean_square + 1e-05) * gain

    tokens = tokens_ref[...].astype(F32)
    normed = rms(tokens, attn_gain_ref[...].astype(F32).reshape(1, width))
    ag[t] = pack_rows(normed[None])[0]
    lane = lax.broadcasted_iota(jnp.int32, (tok, 128), 1)
    dense = jnp.zeros((tok, 128), F32)
    for k in range(ids_ref.shape[1]):
        dense = dense + jnp.where(ids_ref[:, k : k + 1] == lane, gates_ref[:, k : k + 1], 0.0)
    gate_grid[c, x, y, z] = dense
    pl.semaphore_wait(barrier, T + S - 2)
    far_first = (NZ // 2, 1, *range(NZ // 2 + 1, NZ), *range(2, NZ // 2))
    ag_z = {
        k: send(ag.at[t], ag.at[t], ag_ss.at[k], ag_rs.at[k], to_z(k)) for k in far_first
    }

    def ag_hand(k):
        block = ag.at[((z - k + NZ) % NZ) * 2 + y]
        return send(block, block, ag_ss.at[NZ + k], ag_rs.at[NZ + k], peer_y)

    ag_y = [ag_hand(0)]
    gg_z = [
        send(gate_grid.at[c, x, y, z], gate_grid.at[c, x, y, z], gg_ss.at[k], gg_rs.at[k], to_z(k))
        for k in range(1, NZ)
    ]
    for k in (1, NZ - 1, *range(2, NZ - 1)):
        ag_z[k].wait_recv()
        ag_y.append(ag_hand(k))
    for copy in ag_y:
        copy.wait_recv()
    rows = unpack_rows(ag[...]).astype(BF16)
    loads[0].wait()
    proj_q = jnp.dot(rows, wqkv[0], preferred_element_type=F32)
    proj_k = jnp.dot(rows, wqkv[1], preferred_element_type=F32)

    ones = jnp.ones((8, cols), F32)
    nt = (((1,), (1,)), ((), ()))
    squares = jnp.concatenate([proj_q * proj_q, proj_k * proj_k], axis=0)
    sq[t] = lax.dot_general(
        ones, squares, nt, precision=lax.Precision.HIGHEST, preferred_element_type=F32
    )
    sq_copies = [
        send(sq.at[t], sq.at[t], sq_ss.at[k], sq_rs.at[k], to_tensor(k)) for k in range(1, T)
    ]
    for copy in gg_z:
        copy.wait_recv()
    gg_y = send(gate_grid.at[c, x, y], gate_grid.at[c, x, y], gg_ss.at[4], gg_rs.at[4], peer_y)
    proj_v = jnp.dot(rows, wqkv[2], preferred_element_type=F32).astype(BF16)
    values_ref[...] = proj_v
    qv[s, :tok_seq] = (proj_q * q_gain_ref[...].astype(F32).reshape(1, cols)).astype(BF16)
    qv[s, tok_seq:] = proj_v
    qv_copies = [send(qv.at[s], qv.at[s], qv_ss.at[k], qv_rs.at[k], to_seq(k)) for k in range(1, S)]
    for copy in sq_copies:
        copy.wait_recv()
    sums_row = sq[0]
    for k in range(1, T):
        sums_row = sums_row + sq[k]
    sums_grid[s] = sums_row
    sums_copies = [
        send(sums_grid.at[s], sums_grid.at[s], sm_ss.at[k], sm_rs.at[k], to_seq(k))
        for k in range(1, S)
    ]

    def inverse_columns(sums):
        turned = lax.dot_general(
            sums, jnp.full((8, 128), 0.125, F32), (((0,), (0,)), ((), ())),
            precision=lax.Precision.HIGHEST, preferred_element_type=F32,
        )
        return lax.rsqrt(turned / width + 1e-05)[:, :1]

    new_k = (
        proj_k * inverse_columns(sums_row)[tok_seq:] * k_gain_ref[...].astype(F32).reshape(1, cols)
    ).astype(BF16)
    keys_ref[...] = new_k
    ks[s] = new_k
    ks_copies = [send(ks.at[s], ks.at[s], ks_ss.at[k], ks_rs.at[k], to_seq(k)) for k in range(1, S)]
    gg_y.wait_recv()
    gg_x = send(gate_grid.at[c, x], gate_grid.at[c, x], gg_ss.at[5], gg_rs.at[5], peer_x)
    seg_row = seg_row_ref[...]
    owner_row = jnp.zeros(seg_row.shape, jnp.int32)
    for r in range(request_ref.shape[0]):
        slot = jnp.int32(0)
        for g in range(slot_ref.shape[0]):
            slot = jnp.where(request_ref[r] == g, slot_ref[g], slot)
        owner_row = jnp.where(seg_row == r, slot, owner_row)
    chip_tok = 2 * tok_seq
    own_chip, next_chip = x, 1 - x

    def masks(chip):
        pos_q = lax.broadcasted_iota(jnp.int32, (chip_tok, total_tok), 0) + chip * chip_tok
        pos_k = lax.broadcasted_iota(jnp.int32, (chip_tok, total_tok), 1)

        def as_column(row):
            wide = jnp.where(pos_q == pos_k, row.astype(F32), 0.0)
            return jnp.sum(wide, axis=-1, keepdims=True).astype(jnp.int32)

        mask = (as_column(seg_row) == seg_row) & (pos_k <= pos_q)
        return mask, as_column(owner_row) == s

    def queries_of(chip):
        rows = qv[pl.ds(2 * chip, 2), :tok_seq].reshape(chip_tok, cols)
        sums = sums_grid[pl.ds(2 * chip, 2)]
        scale = jnp.concatenate([inverse_columns(sums[k])[:tok_seq] for k in range(2)], axis=0)
        return rows, scale * HD ** (-0.5)

    def prefix_part(rows, scale):
        parts = []
        for h in range(cols // HD):
            part = slice(h * HD, (h + 1) * HD)
            pre = lax.dot_general(rows[:, part], pk[:, part], nt, preferred_element_type=F32)
            pre = pre * scale
            top = jnp.max(pre, axis=-1, keepdims=True)
            pre = jnp.exp(pre - top)
            total = jnp.sum(pre, axis=-1, keepdims=True)
            mix = jnp.dot(pre.astype(BF16), pv[:, part], preferred_element_type=F32)
            parts.append((top, total, mix))
        return parts

    def with_suffix(chip, rows, scale, parts, mask, mine):
        all_v = qv[:, tok_seq:].reshape(total_tok, cols)
        all_k = ks[...].reshape(total_tok, cols)
        heads = []
        for h in range(cols // HD):
            part = slice(h * HD, (h + 1) * HD)
            top_p, total_p, mix_p = parts[h]
            suf = lax.dot_general(rows[:, part], all_k[:, part], nt, preferred_element_type=F32)
            suf = jnp.where(mask, suf * scale, -1e30)
            top = jnp.maximum(top_p, jnp.max(suf, axis=-1, keepdims=True))
            suf = jnp.where(mask, jnp.exp(suf - top), 0.0)
            factor = jnp.exp(top_p - top)
            total = total_p * factor + jnp.sum(suf, axis=-1, keepdims=True)
            mix = jnp.dot(suf.astype(BF16), all_v[:, part], preferred_element_type=F32)
            mix = mix_p * factor + mix
            heads.append(jnp.where(mine, mix / total, 0.0).astype(BF16))
        out = jnp.concatenate(heads, axis=-1).reshape(2, tok_seq, cols)
        att_snd[pl.ds(2 * chip, 2)] = out

    mask_own, mine_own = masks(own_chip)
    mask_next, mine_next = masks(next_chip)
    loads[1].wait()
    loads[2].wait()
    qv_copies[0].wait_recv()
    sums_copies[0].wait_recv()
    rows_own, scale_own = queries_of(own_chip)
    parts_own = prefix_part(rows_own, scale_own)
    for copy in qv_copies[1:] + sums_copies[1:]:
        copy.wait_recv()
    rows_next, scale_next = queries_of(next_chip)
    parts_next = prefix_part(rows_next, scale_next)
    for copy in ks_copies:
        copy.wait_recv()

    def send_attended(d):
        return send(att_snd.at[seq_peer(d)], att_in.at[d], att_ss.at[d], att_rs.at[d], to_seq(d))

    with_suffix(next_chip, rows_next, scale_next, parts_next, mask_next, mine_next)
    far_copies = [send_attended(2), send_attended(3)]
    with_suffix(own_chip, rows_own, scale_own, parts_own, mask_own, mine_own)
    att_copies = [send_attended(1)] + far_copies
    gg_x.wait_recv()
    gg_c = send(gate_grid.at[c], gate_grid.at[c], gg_ss.at[6], gg_rs.at[6], peer_c)
    attended = att_snd[s].astype(F32)
    for k in range(1, S):
        att_copies[k - 1].wait_recv()
        attended = attended + att_in[k].astype(F32)
    loads[3].wait()
    partial = jnp.dot(attended.astype(BF16), wout[...], preferred_element_type=F32)
    rs_snd[...] = pack_rows(partial.reshape(T, tok, width))
    def over_y(k):
        z_to = (z + k) % NZ
        return send(
            rs_snd.at[z_to * 2 + 1 - y], rs_in.at[z_to], rs_ss.at[k], rs_rs.at[k], peer_y
        )

    def over_z(k):
        mid = ((z + k) % NZ) * 2 + y
        return send(rs_snd.at[mid], rs_in.at[NZ + k], rs_ss.at[NZ + k], rs_rs.at[NZ + k], to_z(k))

    rs_y = {k: over_y(k) for k in (*far_first, 0)}
    rs_z = []
    for k in far_first:
        rs_y[k].wait_recv()
        z_to = (z + k) % NZ
        mid = rs_snd[z_to * 2 + y].astype(F32) + rs_in[z_to].astype(F32)
        rs_snd[z_to * 2 + y] = mid.astype(BF16)
        rs_z.append(over_z(k))
    rs_y[0].wait_recv()
    attn_sum = rs_snd[t].astype(F32) + rs_in[z].astype(F32)
    for copy in rs_z:
        copy.wait_recv()
    for k in range(1, NZ):
        attn_sum = attn_sum + rs_in[NZ + k].astype(F32)
    attn_sum = jnp.concatenate([attn_sum[:tok], attn_sum[tok:]], axis=-1)
    mixed = (tokens + attn_sum).astype(BF16).astype(F32)
    expert_in = rms(mixed, mlp_gain_ref[...].astype(F32).reshape(1, width))

    half = width // 2
    grid_a[c, x, y, z] = pack_rows(expert_in[None, :, :half])[0]
    grid_b[c, y, x, z] = pack_rows(expert_in[None, :, half:])[0]
    mine_a, mine_b = grid_a.at[c, x, y, z], grid_b.at[c, y, x, z]

    def z_stage(own, ss, rs):
        return [send(own, own, ss.at[k], rs.at[k], to_z(k)) for k in range(1, NZ)]

    def hand_block(grid, i, j, k, ss, rs, to):
        block = grid.at[c, i, j, (z - k + NZ) % NZ]
        return send(block, block, ss.at[4 + k], rs.at[4 + k], to)

    z_a = z_stage(mine_a, ga_ss, ga_rs)
    z_b = z_stage(mine_b, gb_ss, gb_rs)
    two_a = [hand_block(grid_a, x, y, 0, ga_ss, ga_rs, peer_y)]
    two_b = [hand_block(grid_b, y, x, 0, gb_ss, gb_rs, peer_x)]
    for k in (1, NZ - 1, *range(2, NZ - 1)):
        z_a[k - 1].wait_recv()
        two_a.append(hand_block(grid_a, x, y, k, ga_ss, ga_rs, peer_y))
        z_b[k - 1].wait_recv()
        two_b.append(hand_block(grid_b, y, x, k, gb_ss, gb_rs, peer_x))

    def hand_row(grid, i, j, n, ss, rs, to):
        row = grid.at[c, i, j]
        return send(row, row, ss.at[n], rs.at[n], to)

    one_a = [hand_row(grid_a, x, y, 8, ga_ss, ga_rs, peer_x)]
    one_b = [hand_row(grid_b, y, x, 8, gb_ss, gb_rs, peer_y)]
    for copy in two_a:
        copy.wait_recv()
    one_a.append(hand_row(grid_a, x, 1 - y, 9, ga_ss, ga_rs, peer_x))
    core_a = [send(grid_a.at[c, x], grid_a.at[c, x], ga_ss.at[10], ga_rs.at[10], peer_c)]
    for copy in two_b:
        copy.wait_recv()
    one_b.append(hand_row(grid_b, y, 1 - x, 9, gb_ss, gb_rs, peer_y))
    core_b = [send(grid_b.at[c, y], grid_b.at[c, y], gb_ss.at[10], gb_rs.at[10], peer_c)]
    for copy in one_a:
        copy.wait_recv()
    core_a.append(send(grid_a.at[c, 1 - x], grid_a.at[c, 1 - x], ga_ss.at[11], ga_rs.at[11], peer_c))
    for copy in one_b:
        copy.wait_recv()
    core_b.append(send(grid_b.at[c, 1 - y], grid_b.at[c, 1 - y], gb_ss.at[11], gb_rs.at[11], peer_c))
    for load in loads[4:]:
        load.wait()
    gg_c.wait_recv()
    expert = exp_local * t + s // (S // exp_local)
    blocks = 4 * NZ

    def activity(side):
        block_a = grid_a[side].reshape(blocks, 2 * tok, half // 2)
        raw_b = grid_b[side]
        block_b = jnp.concatenate([raw_b[j, i] for i in range(2) for j in range(2)], axis=0)
        inputs = jnp.concatenate([unpack_rows(block_a), unpack_rows(block_b)], axis=-1).astype(BF16)
        gated = jnp.dot(inputs, wg[...], preferred_element_type=F32)
        upward = jnp.dot(inputs, wu[...], preferred_element_type=F32)
        act = (gated / (1.0 + jnp.exp(-gated)) * upward).astype(BF16)
        table = gate_grid[side].reshape(blocks * tok, 128)
        lanes = lax.broadcasted_iota(jnp.int32, table.shape, 1)
        return act, jnp.sum(jnp.where(lanes == expert, table, 0.0), axis=-1, keepdims=True)

    def down_a(side, act, scale):
        result = jnp.dot(act, wd[:, :half], preferred_element_type=F32) * scale
        packed = pack_rows(result.reshape(blocks, tok, half))
        res_a[side] = packed.reshape(2, 2, NZ, 2 * tok, half // 2)

    def down_b(side, act, scale):
        result = jnp.dot(act, wd[:, half:], preferred_element_type=F32) * scale
        packed = pack_rows(result.reshape(blocks, tok, half))
        for i in range(2):
            for j in range(2):
                first = (i * 2 + j) * NZ
                res_b[side, j, i] = packed[first : first + NZ]

    act_own, scale_own = activity(c)
    for copy in core_a + core_b:
        copy.wait_recv()
    act, scale = activity(1 - c)
    down_a(1 - c, act, scale)
    rcore_a = send(res_a.at[1 - c], rc_a, ra_ss.at[0], ra_rs.at[0], peer_c)
    down_b(1 - c, act, scale)
    rcore_b = send(res_b.at[1 - c], rc_b, rb_ss.at[0], rb_rs.at[0], peer_c)
    down_a(c, act_own, scale_own)
    down_b(c, act_own, scale_own)

    def added(first, second):
        return (first.astype(F32) + second.astype(F32)).astype(BF16)

    rcore_a.wait_recv()
    s1_a[...] = added(res_a[c], rc_a[...])

    def row_out(s1, r1, i, j, n, ss, rs, to):
        return send(s1.at[1 - i, j], r1.at[j], ss.at[n], rs.at[n], to)

    rone_a = [row_out(s1_a, r1_a, x, 1 - y, 1, ra_ss, ra_rs, peer_x)]
    rone_a.append(row_out(s1_a, r1_a, x, y, 2, ra_ss, ra_rs, peer_x))
    rcore_b.wait_recv()
    s1_b[...] = added(res_b[c], rc_b[...])
    rone_b = [row_out(s1_b, r1_b, y, 1 - x, 1, rb_ss, rb_rs, peer_y)]
    rone_b.append(row_out(s1_b, r1_b, y, x, 2, rb_ss, rb_rs, peer_y))
    rone_a[0].wait_recv()
    s2_a[1 - y] = added(s1_a[x, 1 - y], r1_a[1 - y])
    rtwo_a = send(s2_a.at[1 - y], r2_a, ra_ss.at[3], ra_rs.at[3], peer_y)
    rone_b[0].wait_recv()
    s2_b[1 - x] = added(s1_b[y, 1 - x], r1_b[1 - x])
    rtwo_b = send(s2_b.at[1 - x], r2_b, rb_ss.at[3], rb_rs.at[3], peer_x)
    rone_a[1].wait_recv()
    s2_a[y] = added(s1_a[x, y], r1_a[y])
    rone_b[1].wait_recv()
    s2_b[x] = added(s1_b[y, x], r1_b[x])

    def z_out(s3, r3, k, ss, rs):
        return send(s3.at[(z + k) % NZ], r3.at[k], ss.at[3 + k], rs.at[3 + k], to_z(k))

    rtwo_a.wait_recv()
    s3_a[...] = added(s2_a[y], r2_a[...])
    rz_a = [z_out(s3_a, r3_a, k, ra_ss, ra_rs) for k in range(1, NZ)]
    rtwo_b.wait_recv()
    s3_b[...] = added(s2_b[x], r2_b[...])
    rz_b = [z_out(s3_b, r3_b, k, rb_ss, rb_rs) for k in range(1, NZ)]
    sum_a = s3_a[z].astype(F32)
    sum_b = s3_b[z].astype(F32)
    for k in range(1, NZ):
        rz_a[k - 1].wait_recv()
        sum_a = sum_a + r3_a[k].astype(F32)
    for k in range(1, NZ):
        rz_b[k - 1].wait_recv()
        sum_b = sum_b + r3_b[k].astype(F32)
    moe = jnp.concatenate([sum_a[:tok], sum_a[tok:], sum_b[:tok], sum_b[tok:]], axis=-1)
    out_ref[...] = (mixed + moe).astype(BF16)
    for copy in started:
        copy.wait_send()


def local_kernel(
    tokens, attn_gain, w_qkv, q_gain, k_gain, w_out, prefix_keys, prefix_values, segments,
    request_group, prefix_owner, mlp_gain, expert_ids, gate_weights, w_gate, w_up, w_down,
):
    S, T = lax.axis_size("seq"), lax.axis_size("tensor")
    NZ = T // 2
    tok, width = tokens.shape
    cols = w_qkv.shape[2]
    tok_seq = tok * T
    slots = prefix_keys.shape[1]
    units = w_gate.shape[2]
    vm, dma = pltpu.VMEM, pltpu.SemaphoreType.DMA
    quarter = width // 4
    blk = (2 * tok, quarter)
    grid = vm((2, 2, 2, NZ) + blk, BF16)
    pair = lambda *lead: [vm(lead + blk, BF16)] * 2
    scratch = [
        vm((3, width, cols), BF16), vm((cols, width), BF16),
        vm((slots, cols), BF16), vm((slots, cols), BF16),
        vm((width, units), BF16), vm((width, units), BF16), vm((units, width), BF16),
        vm((T, 2 * tok, width // 2), BF16), vm((T, 8, 2 * tok_seq), F32),
        vm((S, 8, 2 * tok_seq), F32), vm((S, 2 * tok_seq, cols), BF16),
        *[vm((S, tok_seq, cols), BF16)] * 3,
        vm((T, 2 * tok, width // 2), BF16), vm((T, 2 * tok, width // 2), BF16),
        grid, grid, vm((2, 2, 2, NZ, tok, 128), F32),
        grid, grid,
        *pair(2, 2, NZ), *pair(2, 2, NZ), *pair(2, NZ),
        *pair(2, NZ), *pair(NZ), *pair(NZ), *pair(NZ),
        dma((7,)),
        *[dma((T,))] * 4, *[dma((S,))] * 8, *[dma((T,))] * 2,
        *[dma((8,))] * 2, *[dma((NZ + 8,))] * 8,
    ]
    in_vmem = pl.BlockSpec(memory_space=pltpu.VMEM)
    in_smem = pl.BlockSpec(memory_space=pltpu.SMEM)
    in_any = pl.BlockSpec(memory_space=pl.ANY)
    results = pl.pallas_call(
        functools.partial(layer_kernel, (S, T, NZ, EXP_DEV)),
        out_shape=(
            jax.ShapeDtypeStruct((tok, width), BF16),
            jax.ShapeDtypeStruct((tok_seq, cols), BF16),
            jax.ShapeDtypeStruct((tok_seq, cols), BF16),
        ),
        in_specs=[in_vmem] * 6 + [in_smem] * 2 + [in_vmem] * 2 + [in_any] * 7,
        out_specs=(in_vmem,) * 3,
        scratch_shapes=scratch,
        compiler_params=pltpu.CompilerParams(
            collective_id=0, has_side_effects=True, vmem_limit_bytes=56 * 2**20
        ),
    )(
        tokens, attn_gain, q_gain, k_gain, mlp_gain,
        segments[None], request_group, prefix_owner, expert_ids, gate_weights,
        jnp.transpose(w_qkv, (1, 0, 2)), w_out, prefix_keys, prefix_values, w_gate, w_up, w_down,
    )
    return pl.pallas_call(
        hand_on,
        out_shape=tuple(jax.ShapeDtypeStruct(r.shape, r.dtype) for r in results),
        in_specs=[in_vmem] * 3,
        out_specs=(in_vmem,) * 3,
    )(*results)


def hand_on(*refs):
    for source, target in zip(refs[:3], refs[3:]):
        target[...] = source[...]


def whole_heads(*arrays):
    seq_size, tensor_size = lax.axis_size("seq"), lax.axis_size("tensor")
    if arrays[2].shape[2] % HD == 0 and seq_size == 4 and tensor_size == 8:
        return local_kernel(*arrays)
    return local(*arrays)


def solution(mesh):
    return jax.shard_map(
        whole_heads,
        mesh=mesh,
        in_specs=(
            P(("seq", "tensor"), None),
            P(),
            P(None, None, "tensor"),
            P("tensor"),
            P("tensor"),
            P("tensor", None),
            P("seq", None, "tensor"),
            P("seq", None, "tensor"),
            P(),
            P(),
            P(),
            P(),
            P(("seq", "tensor"), None),
            P(("seq", "tensor"), None),
            P(("tensor", "seq"), None, None),
            P(("tensor", "seq"), None, None),
            P(("tensor", "seq"), None, None),
        ),
        out_specs=(P(("seq", "tensor"), None), P("seq", "tensor"), P("seq", "tensor")),
        check_vma=False,
    )
```

```python
import functools

import jax
import jax.numpy as jnp
from jax import lax
from jax.experimental import pallas as pl
from jax.experimental.pallas import tpu as pltpu
from jax.sharding import PartitionSpec as P

HD = 128
TOP = 8
EXP_DEV = 2


def from_partner(value, axis, stride):
    mask = 2**stride
    pairs = [(source, source ^ mask) for source in range(lax.axis_size(axis))]
    return lax.ppermute(value, axis, pairs)


def passed_along(value, axis, by):
    devices = lax.axis_size(axis)
    pairs = [(i, i + by) for i in range(devices) if 0 <= i + by < devices]
    return lax.ppermute(value, axis, pairs)


def rms_scale(values, gain):
    mean_square = jnp.mean(values * values, axis=-1, keepdims=True)
    return values * lax.rsqrt(mean_square + 1e-05) * gain.astype(jnp.float32)


def attend_block(carry, queries_heads, block, mask):
    largest, total, accum = carry
    heads_local = queries_heads.shape[1]
    count = block.shape[0]
    key_block = block[:, 0].reshape(count, heads_local, HD)
    value_block = block[:, 1].reshape(count, heads_local, HD)
    scores = jnp.einsum(
        "qhd,khd->hqk", queries_heads, key_block, preferred_element_type=jnp.float32
    ) * HD ** (-0.5)
    scores = jnp.where(mask[None], scores, -1e30)
    new_largest = jnp.maximum(largest, jnp.max(scores, axis=-1))
    weights = jnp.where(mask[None], jnp.exp(scores - new_largest[:, :, None]), 0.0)
    factor = jnp.exp(largest - new_largest)
    total = total * factor + jnp.sum(weights, axis=-1)
    update = jnp.einsum(
        "hqk,khd->hqd",
        weights.astype(jnp.bfloat16),
        value_block,
        preferred_element_type=jnp.float32,
    )
    accum = accum * factor[:, :, None] + update
    return (new_largest, total, accum)


def local(
    tokens,
    attn_gain,
    w_qkv,
    q_gain,
    k_gain,
    w_out,
    prefix_keys,
    prefix_values,
    segments,
    request_group,
    prefix_owner,
    mlp_gain,
    expert_ids,
    gate_weights,
    w_gate,
    w_up,
    w_down,
):
    tensor_size = lax.axis_size("tensor")
    seq_size = lax.axis_size("seq")
    seq_index = lax.axis_index("seq")
    tensor_index = lax.axis_index("tensor")
    tok_dev = tokens.shape[0]
    width = tokens.shape[1]
    tok_seq = tok_dev * tensor_size
    columns = w_qkv.shape[2]
    paired = columns < HD
    normed = rms_scale(tokens.astype(jnp.float32), attn_gain).astype(jnp.bfloat16)
    w_flat = w_qkv.reshape(width, 3 * columns)
    projected = jnp.dot(
        lax.all_gather(normed, "tensor", axis=0, tiled=True),
        w_flat,
        preferred_element_type=jnp.float32,
    )
    query_part = projected[:, :columns]
    key_part = projected[:, columns : 2 * columns]
    squares = lax.psum(
        (jnp.sum(query_part * query_part, axis=-1), jnp.sum(key_part * key_part, axis=-1)), "tensor"
    )
    query_rows = (
        query_part * lax.rsqrt(squares[0] / width + 1e-05)[:, None] * q_gain.astype(jnp.float32)
    ).astype(jnp.bfloat16)
    new_keys = (
        key_part * lax.rsqrt(squares[1] / width + 1e-05)[:, None] * k_gain.astype(jnp.float32)
    ).astype(jnp.bfloat16)
    new_values = projected[:, 2 * columns :].astype(jnp.bfloat16)
    stacked = jnp.stack(
        [
            jnp.concatenate([new_keys, prefix_keys[0]], axis=0),
            jnp.concatenate([new_values, prefix_values[0]], axis=0),
        ],
        axis=1,
    )
    half_rows = tok_seq // 2
    if paired:
        lower_bit = tensor_index % 2
        partner = from_partner(stacked, "tensor", 0)
        full = jnp.where(
            lower_bit == 0,
            jnp.concatenate([stacked, partner], axis=-1),
            jnp.concatenate([partner, stacked], axis=-1),
        )
        query_halves = query_rows.reshape(2, half_rows, columns)
        own_half = lax.dynamic_index_in_dim(query_halves, lower_bit, 0, keepdims=False)
        send_half = lax.dynamic_index_in_dim(query_halves, 1 - lower_bit, 0, keepdims=False)
        got_half = from_partner(send_half, "tensor", 0)
        query_full = jnp.where(
            lower_bit == 0,
            jnp.concatenate([own_half, got_half], axis=-1),
            jnp.concatenate([got_half, own_half], axis=-1),
        )
        query_count = half_rows
        query_offset = lower_bit * half_rows
        heads_local = 1
    else:
        full = stacked
        query_full = query_rows
        query_count = tok_seq
        query_offset = jnp.int32(0)
        heads_local = columns // HD
    suffix_full = full[:tok_seq]
    prefix_full = full[tok_seq:]
    queries_heads = query_full.reshape(query_count, heads_local, HD)
    groups_count = prefix_owner.shape[0]
    request_count = request_group.shape[0]
    token_group = jnp.sum(
        jnp.where(
            segments[:, None] == jnp.arange(request_count, dtype=jnp.int32)[None, :],
            request_group[None, :],
            0,
        ),
        axis=1,
    )
    base_row = seq_index * tok_seq
    query_start = base_row + query_offset
    query_seg = lax.dynamic_slice_in_dim(segments, query_start, query_count, 0)
    query_group = lax.dynamic_slice_in_dim(token_group, query_start, query_count, 0)
    query_pos = query_start + jnp.arange(query_count, dtype=jnp.int32)
    padded_seg = jnp.concatenate([jnp.full((tok_seq,), -1, jnp.int32), segments], axis=0)
    key_seg = lax.dynamic_slice_in_dim(padded_seg, base_row, 2 * tok_seq, 0)
    key_pos = base_row - tok_seq + jnp.arange(2 * tok_seq, dtype=jnp.int32)
    previous = passed_along(suffix_full, "seq", 1)
    suffix_keys = jnp.concatenate([previous, suffix_full], axis=0)
    suffix_mask = (key_seg[None, :] == query_seg[:, None]) & (
        key_pos[None, :] <= query_pos[:, None]
    )
    carry = (
        jnp.full((heads_local, query_count), -1e30, jnp.float32),
        jnp.zeros((heads_local, query_count), jnp.float32),
        jnp.zeros((heads_local, query_count, HD), jnp.float32),
    )
    carry = attend_block(carry, queries_heads, suffix_keys, suffix_mask)
    owner_of_query = jnp.sum(
        jnp.where(
            query_group[:, None] == jnp.arange(groups_count, dtype=jnp.int32)[None, :],
            prefix_owner[None, :],
            0,
        ),
        axis=1,
    )
    state = carry
    piece = lax.all_gather(prefix_full[None], "seq", axis=0, tiled=True)
    start = jnp.int32(0)
    for offset in range(piece.shape[0]):
        slot_mask = (owner_of_query == start + offset)[:, None]
        state = attend_block(state, queries_heads, piece[offset], slot_mask)
    carry = state
    attended = (carry[2] / carry[1][:, :, None]).astype(jnp.bfloat16)
    attended = jnp.transpose(attended, (1, 0, 2)).reshape(query_count, heads_local * HD)
    if paired:
        split_out = attended.reshape(query_count, 2, columns)
        own_out = lax.dynamic_index_in_dim(split_out, lower_bit, 1, keepdims=False)
        send_out = lax.dynamic_index_in_dim(split_out, 1 - lower_bit, 1, keepdims=False)
        got_out = from_partner(send_out, "tensor", 0)
        attended_local = jnp.where(
            lower_bit == 0,
            jnp.concatenate([own_out, got_out], axis=0),
            jnp.concatenate([got_out, own_out], axis=0),
        )
    else:
        attended_local = attended
    attn_sum = lax.psum_scatter(
        jnp.dot(attended_local, w_out, preferred_element_type=jnp.float32).astype(jnp.bfloat16),
        "tensor",
        scatter_dimension=0,
        tiled=True,
    ).astype(jnp.float32)
    mixed_rows = (tokens.astype(jnp.float32) + attn_sum).astype(jnp.bfloat16)
    expert_in = rms_scale(mixed_rows.astype(jnp.float32), mlp_gain).astype(jnp.bfloat16)
    exp_local = EXP_DEV
    experts_all = exp_local * tensor_size
    own_expert = seq_index // (seq_size // exp_local)
    capacity = max(2, 2 * tok_dev * TOP // experts_all)
    flat_ids = expert_ids.reshape(-1)
    onehot = (flat_ids[:, None] == jnp.arange(experts_all, dtype=jnp.int32)[None, :]).astype(
        jnp.int32
    )
    before = jnp.cumsum(onehot, axis=0) - onehot
    slot = flat_ids * capacity + jnp.sum(before * onehot, axis=1)
    slot_match = (
        slot.reshape(tok_dev, TOP)[:, :, None]
        == jnp.arange(experts_all * capacity, dtype=jnp.int32)[None, None, :]
    )
    dispatch_table = jnp.transpose(jnp.any(slot_match, axis=1)).astype(jnp.bfloat16)
    combine_table = jnp.sum(jnp.where(slot_match, gate_weights[:, :, None], 0.0), axis=1)
    buffer = jnp.dot(dispatch_table, expert_in, preferred_element_type=jnp.float32).astype(
        jnp.bfloat16
    )
    buffer = buffer.reshape(tensor_size, exp_local, capacity, width)
    received = lax.all_to_all(buffer, "tensor", split_axis=0, concat_axis=0, tiled=True)
    gate_local = w_gate[0]
    up_local = w_up[0]
    down_local = w_down[0]
    keep_expert = (jnp.arange(exp_local, dtype=jnp.int32) == own_expert)[None, None, :, None, None]
    chosen = lax.dynamic_index_in_dim(
        lax.all_gather(received[None], "seq", axis=0, tiled=True), own_expert, 2, keepdims=False
    )
    gated = jnp.einsum("srcd,df->srcf", chosen, gate_local, preferred_element_type=jnp.float32)
    upward = jnp.einsum("srcd,df->srcf", chosen, up_local, preferred_element_type=jnp.float32)
    activity = (jax.nn.silu(gated) * upward).astype(jnp.bfloat16)
    result = jnp.einsum("srcf,fd->srcd", activity, down_local, preferred_element_type=jnp.float32)
    partials = jnp.where(keep_expert, result[:, :, None], 0.0)
    summed = lax.psum_scatter(
        partials.astype(jnp.bfloat16), "seq", scatter_dimension=0, tiled=True
    ).astype(jnp.float32)
    returned = lax.all_to_all(
        summed[0].astype(jnp.bfloat16), "tensor", split_axis=0, concat_axis=0, tiled=True
    ).astype(jnp.float32)
    moe_sum = jnp.dot(
        combine_table,
        returned.reshape(experts_all * capacity, width),
        preferred_element_type=jnp.float32,
        precision=lax.Precision.HIGHEST,
    )
    output = (mixed_rows.astype(jnp.float32) + moe_sum).astype(jnp.bfloat16)
    return (output, new_keys, new_values)


MESH = pl.DeviceIdType.MESH
F32 = jnp.float32
BF16 = jnp.bfloat16


def pack_rows(value):
    half = value.shape[-1] // 2
    return jnp.concatenate([value[:, :, :half], value[:, :, half:]], axis=1).astype(BF16)


def unpack_rows(value):
    count, rows, half = value.shape
    wide = value.astype(F32).reshape(count, 2, rows // 2, half)
    left = wide[:, 0].reshape(count * (rows // 2), half)
    right = wide[:, 1].reshape(count * (rows // 2), half)
    return jnp.concatenate([left, right], axis=-1)


def layer_kernel(
    dims,
    tokens_ref, attn_gain_ref, q_gain_ref, k_gain_ref, mlp_gain_ref,
    seg_row_ref, request_ref, slot_ref, ids_ref, gates_ref,
    wqkv_hbm, wout_hbm, pk_hbm, pv_hbm, wg_hbm, wu_hbm, wd_hbm,
    out_ref, keys_ref, values_ref,
    wqkv, wout, pk, pv, wg, wu, wd,
    ag, sq, sums_grid, qv, ks, att_snd, att_in, rs_snd, rs_in,
    grid_a, grid_b, gate_grid,
    res_a, res_b, rc_a, rc_b, s1_a, s1_b, r1_a, r1_b,
    s2_a, s2_b, r2_a, r2_b, s3_a, s3_b, r3_a, r3_b,
    w_sem,
    ag_ss, ag_rs, sq_ss, sq_rs, qv_ss, qv_rs, ks_ss, ks_rs, sm_ss, sm_rs, att_ss, att_rs, rs_ss, rs_rs,
    gg_ss, gg_rs, ga_ss, ga_rs, gb_ss, gb_rs, ra_ss, ra_rs, rb_ss, rb_rs,
):
    S, T, NZ, exp_local = dims
    s = lax.axis_index("seq")
    t = lax.axis_index("tensor")
    x, c = s // 2, s % 2
    z, y = t // 2, t % 2
    tok, width = tokens_ref.shape
    cols = keys_ref.shape[1]
    tok_seq = tok * T
    total_tok = tok_seq * S
    started = []

    loads = [
        pltpu.make_async_copy(wqkv_hbm, wqkv, w_sem.at[0]),
        pltpu.make_async_copy(pk_hbm.at[0], pk, w_sem.at[1]),
        pltpu.make_async_copy(pv_hbm.at[0], pv, w_sem.at[2]),
        pltpu.make_async_copy(wout_hbm, wout, w_sem.at[3]),
        pltpu.make_async_copy(wg_hbm.at[0], wg, w_sem.at[4]),
        pltpu.make_async_copy(wu_hbm.at[0], wu, w_sem.at[5]),
        pltpu.make_async_copy(wd_hbm.at[0], wd, w_sem.at[6]),
    ]
    for load in loads:
        load.start()

    barrier = pltpu.get_barrier_semaphore()
    for k in range(1, T):
        pl.semaphore_signal(barrier, inc=1, device_id=(s, (t + k) % T), device_id_type=MESH)
    for k in range(1, S):
        pl.semaphore_signal(barrier, inc=1, device_id=((s + k) % S, t), device_id_type=MESH)

    def send(src, dst, send_sem, recv_sem, to):
        copy = pltpu.make_async_remote_copy(
            src_ref=src, dst_ref=dst, send_sem=send_sem, recv_sem=recv_sem,
            device_id=to, device_id_type=MESH,
        )
        copy.start()
        started.append(copy)
        return copy

    def to_tensor(k):
        return (s, (t + k) % T)

    def seq_peer(d):
        return ((x + d // 2) % 2) * 2 + (c + d % 2) % 2

    def to_seq(d):
        return (seq_peer(d), t)

    peer_x = ((1 - x) * 2 + c, t)
    peer_c = (x * 2 + 1 - c, t)
    peer_y = (s, z * 2 + 1 - y)

    def to_z(k):
        return (s, ((z + k) % NZ) * 2 + y)

    def rms(value, gain):
        mean_square = jnp.mean(value * value, axis=-1, keepdims=True)
        return value * lax.rsqrt(mean_square + 1e-05) * gain

    tokens = tokens_ref[...].astype(F32)
    normed = rms(tokens, attn_gain_ref[...].astype(F32).reshape(1, width))
    ag[t] = pack_rows(normed[None])[0]
    lane = lax.broadcasted_iota(jnp.int32, (tok, 128), 1)
    dense = jnp.zeros((tok, 128), F32)
    for k in range(ids_ref.shape[1]):
        dense = dense + jnp.where(ids_ref[:, k : k + 1] == lane, gates_ref[:, k : k + 1], 0.0)
    gate_grid[c, x, y, z] = dense
    pl.semaphore_wait(barrier, T + S - 2)
    far_first = sorted(range(1, T), key=lambda k: abs(k - T // 2))
    ag_copies = [
        send(ag.at[t], ag.at[t], ag_ss.at[k], ag_rs.at[k], to_tensor(k)) for k in far_first
    ]
    gg_z = [
        send(gate_grid.at[c, x, y, z], gate_grid.at[c, x, y, z], gg_ss.at[k], gg_rs.at[k], to_z(k))
        for k in range(1, NZ)
    ]
    for copy in ag_copies:
        copy.wait_recv()
    rows = unpack_rows(ag[...]).astype(BF16)
    loads[0].wait()
    proj_q = jnp.dot(rows, wqkv[0], preferred_element_type=F32)
    proj_k = jnp.dot(rows, wqkv[1], preferred_element_type=F32)

    ones = jnp.ones((8, cols), F32)
    nt = (((1,), (1,)), ((), ()))
    squares = jnp.concatenate([proj_q * proj_q, proj_k * proj_k], axis=0)
    sq[t] = lax.dot_general(
        ones, squares, nt, precision=lax.Precision.HIGHEST, preferred_element_type=F32
    )
    sq_copies = [
        send(sq.at[t], sq.at[t], sq_ss.at[k], sq_rs.at[k], to_tensor(k)) for k in range(1, T)
    ]
    for copy in gg_z:
        copy.wait_recv()
    gg_y = send(gate_grid.at[c, x, y], gate_grid.at[c, x, y], gg_ss.at[4], gg_rs.at[4], peer_y)
    proj_v = jnp.dot(rows, wqkv[2], preferred_element_type=F32).astype(BF16)
    values_ref[...] = proj_v
    qv[s, :tok_seq] = (proj_q * q_gain_ref[...].astype(F32).reshape(1, cols)).astype(BF16)
    qv[s, tok_seq:] = proj_v
    qv_copies = [send(qv.at[s], qv.at[s], qv_ss.at[k], qv_rs.at[k], to_seq(k)) for k in range(1, S)]
    for copy in sq_copies:
        copy.wait_recv()
    sums_row = sq[0]
    for k in range(1, T):
        sums_row = sums_row + sq[k]
    sums_grid[s] = sums_row
    sums_copies = [
        send(sums_grid.at[s], sums_grid.at[s], sm_ss.at[k], sm_rs.at[k], to_seq(k))
        for k in range(1, S)
    ]

    def inverse_columns(sums):
        turned = lax.dot_general(
            sums, jnp.full((8, 128), 0.125, F32), (((0,), (0,)), ((), ())),
            precision=lax.Precision.HIGHEST, preferred_element_type=F32,
        )
        return lax.rsqrt(turned / width + 1e-05)[:, :1]

    new_k = (
        proj_k * inverse_columns(sums_row)[tok_seq:] * k_gain_ref[...].astype(F32).reshape(1, cols)
    ).astype(BF16)
    keys_ref[...] = new_k
    ks[s] = new_k
    ks_copies = [send(ks.at[s], ks.at[s], ks_ss.at[k], ks_rs.at[k], to_seq(k)) for k in range(1, S)]
    gg_y.wait_recv()
    gg_x = send(gate_grid.at[c, x], gate_grid.at[c, x], gg_ss.at[5], gg_rs.at[5], peer_x)
    seg_row = seg_row_ref[...]
    owner_row = jnp.zeros(seg_row.shape, jnp.int32)
    for r in range(request_ref.shape[0]):
        slot = jnp.int32(0)
        for g in range(slot_ref.shape[0]):
            slot = jnp.where(request_ref[r] == g, slot_ref[g], slot)
        owner_row = jnp.where(seg_row == r, slot, owner_row)
    chip_tok = 2 * tok_seq
    own_chip, next_chip = x, 1 - x

    def masks(chip):
        pos_q = lax.broadcasted_iota(jnp.int32, (chip_tok, total_tok), 0) + chip * chip_tok
        pos_k = lax.broadcasted_iota(jnp.int32, (chip_tok, total_tok), 1)

        def as_column(row):
            wide = jnp.where(pos_q == pos_k, row.astype(F32), 0.0)
            return jnp.sum(wide, axis=-1, keepdims=True).astype(jnp.int32)

        mask = (as_column(seg_row) == seg_row) & (pos_k <= pos_q)
        return mask, as_column(owner_row) == s

    def queries_of(chip):
        rows = qv[pl.ds(2 * chip, 2), :tok_seq].reshape(chip_tok, cols)
        sums = sums_grid[pl.ds(2 * chip, 2)]
        scale = jnp.concatenate([inverse_columns(sums[k])[:tok_seq] for k in range(2)], axis=0)
        return rows, scale * HD ** (-0.5)

    def prefix_part(rows, scale):
        parts = []
        for h in range(cols // HD):
            part = slice(h * HD, (h + 1) * HD)
            pre = lax.dot_general(rows[:, part], pk[:, part], nt, preferred_element_type=F32)
            pre = pre * scale
            top = jnp.max(pre, axis=-1, keepdims=True)
            pre = jnp.exp(pre - top)
            total = jnp.sum(pre, axis=-1, keepdims=True)
            mix = jnp.dot(pre.astype(BF16), pv[:, part], preferred_element_type=F32)
            parts.append((top, total, mix))
        return parts

    def with_suffix(chip, rows, scale, parts, mask, mine):
        all_v = qv[:, tok_seq:].reshape(total_tok, cols)
        all_k = ks[...].reshape(total_tok, cols)
        heads = []
        for h in range(cols // HD):
            part = slice(h * HD, (h + 1) * HD)
            top_p, total_p, mix_p = parts[h]
            suf = lax.dot_general(rows[:, part], all_k[:, part], nt, preferred_element_type=F32)
            suf = jnp.where(mask, suf * scale, -1e30)
            top = jnp.maximum(top_p, jnp.max(suf, axis=-1, keepdims=True))
            suf = jnp.where(mask, jnp.exp(suf - top), 0.0)
            factor = jnp.exp(top_p - top)
            total = total_p * factor + jnp.sum(suf, axis=-1, keepdims=True)
            mix = jnp.dot(suf.astype(BF16), all_v[:, part], preferred_element_type=F32)
            mix = mix_p * factor + mix
            heads.append(jnp.where(mine, mix / total, 0.0).astype(BF16))
        out = jnp.concatenate(heads, axis=-1).reshape(2, tok_seq, cols)
        att_snd[pl.ds(2 * chip, 2)] = out

    mask_own, mine_own = masks(own_chip)
    mask_next, mine_next = masks(next_chip)
    loads[1].wait()
    loads[2].wait()
    qv_copies[0].wait_recv()
    sums_copies[0].wait_recv()
    rows_own, scale_own = queries_of(own_chip)
    parts_own = prefix_part(rows_own, scale_own)
    for copy in qv_copies[1:] + sums_copies[1:]:
        copy.wait_recv()
    rows_next, scale_next = queries_of(next_chip)
    parts_next = prefix_part(rows_next, scale_next)
    for copy in ks_copies:
        copy.wait_recv()

    def send_attended(d):
        return send(att_snd.at[seq_peer(d)], att_in.at[d], att_ss.at[d], att_rs.at[d], to_seq(d))

    with_suffix(next_chip, rows_next, scale_next, parts_next, mask_next, mine_next)
    far_copies = [send_attended(2), send_attended(3)]
    with_suffix(own_chip, rows_own, scale_own, parts_own, mask_own, mine_own)
    att_copies = [send_attended(1)] + far_copies
    gg_x.wait_recv()
    gg_c = send(gate_grid.at[c], gate_grid.at[c], gg_ss.at[6], gg_rs.at[6], peer_c)
    attended = att_snd[s].astype(F32)
    for k in range(1, S):
        att_copies[k - 1].wait_recv()
        attended = attended + att_in[k].astype(F32)
    loads[3].wait()
    partial = jnp.dot(attended.astype(BF16), wout[...], preferred_element_type=F32)
    rs_snd[...] = pack_rows(partial.reshape(T, tok, width))
    rs_copies = [
        send(rs_snd.at[(t + k) % T], rs_in.at[k], rs_ss.at[k], rs_rs.at[k], to_tensor(k))
        for k in far_first
    ]
    attn_sum = rs_snd[t].astype(F32)
    for copy in rs_copies:
        copy.wait_recv()
    for k in range(1, T):
        attn_sum = attn_sum + rs_in[k].astype(F32)
    attn_sum = jnp.concatenate([attn_sum[:tok], attn_sum[tok:]], axis=-1)
    mixed = (tokens + attn_sum).astype(BF16).astype(F32)
    expert_in = rms(mixed, mlp_gain_ref[...].astype(F32).reshape(1, width))

    half = width // 2
    grid_a[c, x, y, z] = pack_rows(expert_in[None, :, :half])[0]
    grid_b[c, y, x, z] = pack_rows(expert_in[None, :, half:])[0]
    mine_a, mine_b = grid_a.at[c, x, y, z], grid_b.at[c, y, x, z]

    def z_stage(own, ss, rs):
        return [send(own, own, ss.at[k], rs.at[k], to_z(k)) for k in range(1, NZ)]

    def hand_block(grid, i, j, k, ss, rs, to):
        block = grid.at[c, i, j, (z - k + NZ) % NZ]
        return send(block, block, ss.at[4 + k], rs.at[4 + k], to)

    z_a = z_stage(mine_a, ga_ss, ga_rs)
    z_b = z_stage(mine_b, gb_ss, gb_rs)
    two_a = [hand_block(grid_a, x, y, 0, ga_ss, ga_rs, peer_y)]
    two_b = [hand_block(grid_b, y, x, 0, gb_ss, gb_rs, peer_x)]
    for k in (1, NZ - 1, *range(2, NZ - 1)):
        z_a[k - 1].wait_recv()
        two_a.append(hand_block(grid_a, x, y, k, ga_ss, ga_rs, peer_y))
        z_b[k - 1].wait_recv()
        two_b.append(hand_block(grid_b, y, x, k, gb_ss, gb_rs, peer_x))

    def hand_row(grid, i, j, n, ss, rs, to):
        row = grid.at[c, i, j]
        return send(row, row, ss.at[n], rs.at[n], to)

    one_a = [hand_row(grid_a, x, y, 8, ga_ss, ga_rs, peer_x)]
    one_b = [hand_row(grid_b, y, x, 8, gb_ss, gb_rs, peer_y)]
    for copy in two_a:
        copy.wait_recv()
    one_a.append(hand_row(grid_a, x, 1 - y, 9, ga_ss, ga_rs, peer_x))
    core_a = [send(grid_a.at[c, x], grid_a.at[c, x], ga_ss.at[10], ga_rs.at[10], peer_c)]
    for copy in two_b:
        copy.wait_recv()
    one_b.append(hand_row(grid_b, y, 1 - x, 9, gb_ss, gb_rs, peer_y))
    core_b = [send(grid_b.at[c, y], grid_b.at[c, y], gb_ss.at[10], gb_rs.at[10], peer_c)]
    for copy in one_a:
        copy.wait_recv()
    core_a.append(send(grid_a.at[c, 1 - x], grid_a.at[c, 1 - x], ga_ss.at[11], ga_rs.at[11], peer_c))
    for copy in one_b:
        copy.wait_recv()
    core_b.append(send(grid_b.at[c, 1 - y], grid_b.at[c, 1 - y], gb_ss.at[11], gb_rs.at[11], peer_c))
    for load in loads[4:]:
        load.wait()
    gg_c.wait_recv()
    expert = exp_local * t + s // (S // exp_local)
    blocks = 4 * NZ

    def activity(side):
        block_a = grid_a[side].reshape(blocks, 2 * tok, half // 2)
        raw_b = grid_b[side]
        block_b = jnp.concatenate([raw_b[j, i] for i in range(2) for j in range(2)], axis=0)
        inputs = jnp.concatenate([unpack_rows(block_a), unpack_rows(block_b)], axis=-1).astype(BF16)
        gated = jnp.dot(inputs, wg[...], preferred_element_type=F32)
        upward = jnp.dot(inputs, wu[...], preferred_element_type=F32)
        act = (gated / (1.0 + jnp.exp(-gated)) * upward).astype(BF16)
        table = gate_grid[side].reshape(blocks * tok, 128)
        lanes = lax.broadcasted_iota(jnp.int32, table.shape, 1)
        return act, jnp.sum(jnp.where(lanes == expert, table, 0.0), axis=-1, keepdims=True)

    def down_a(side, act, scale):
        result = jnp.dot(act, wd[:, :half], preferred_element_type=F32) * scale
        packed = pack_rows(result.reshape(blocks, tok, half))
        res_a[side] = packed.reshape(2, 2, NZ, 2 * tok, half // 2)

    def down_b(side, act, scale):
        result = jnp.dot(act, wd[:, half:], preferred_element_type=F32) * scale
        packed = pack_rows(result.reshape(blocks, tok, half))
        for i in range(2):
            for j in range(2):
                first = (i * 2 + j) * NZ
                res_b[side, j, i] = packed[first : first + NZ]

    act_own, scale_own = activity(c)
    for copy in core_a + core_b:
        copy.wait_recv()
    act, scale = activity(1 - c)
    down_a(1 - c, act, scale)
    rcore_a = send(res_a.at[1 - c], rc_a, ra_ss.at[0], ra_rs.at[0], peer_c)
    down_b(1 - c, act, scale)
    rcore_b = send(res_b.at[1 - c], rc_b, rb_ss.at[0], rb_rs.at[0], peer_c)
    down_a(c, act_own, scale_own)
    down_b(c, act_own, scale_own)

    def added(first, second):
        return (first.astype(F32) + second.astype(F32)).astype(BF16)

    rcore_a.wait_recv()
    s1_a[...] = added(res_a[c], rc_a[...])

    def row_out(s1, r1, i, j, n, ss, rs, to):
        return send(s1.at[1 - i, j], r1.at[j], ss.at[n], rs.at[n], to)

    rone_a = [row_out(s1_a, r1_a, x, 1 - y, 1, ra_ss, ra_rs, peer_x)]
    rone_a.append(row_out(s1_a, r1_a, x, y, 2, ra_ss, ra_rs, peer_x))
    rcore_b.wait_recv()
    s1_b[...] = added(res_b[c], rc_b[...])
    rone_b = [row_out(s1_b, r1_b, y, 1 - x, 1, rb_ss, rb_rs, peer_y)]
    rone_b.append(row_out(s1_b, r1_b, y, x, 2, rb_ss, rb_rs, peer_y))
    rone_a[0].wait_recv()
    s2_a[1 - y] = added(s1_a[x, 1 - y], r1_a[1 - y])
    rtwo_a = send(s2_a.at[1 - y], r2_a, ra_ss.at[3], ra_rs.at[3], peer_y)
    rone_b[0].wait_recv()
    s2_b[1 - x] = added(s1_b[y, 1 - x], r1_b[1 - x])
    rtwo_b = send(s2_b.at[1 - x], r2_b, rb_ss.at[3], rb_rs.at[3], peer_x)
    rone_a[1].wait_recv()
    s2_a[y] = added(s1_a[x, y], r1_a[y])
    rone_b[1].wait_recv()
    s2_b[x] = added(s1_b[y, x], r1_b[x])

    def z_out(s3, r3, k, ss, rs):
        return send(s3.at[(z + k) % NZ], r3.at[k], ss.at[3 + k], rs.at[3 + k], to_z(k))

    rtwo_a.wait_recv()
    s3_a[...] = added(s2_a[y], r2_a[...])
    rz_a = [z_out(s3_a, r3_a, k, ra_ss, ra_rs) for k in range(1, NZ)]
    rtwo_b.wait_recv()
    s3_b[...] = added(s2_b[x], r2_b[...])
    rz_b = [z_out(s3_b, r3_b, k, rb_ss, rb_rs) for k in range(1, NZ)]
    sum_a = s3_a[z].astype(F32)
    sum_b = s3_b[z].astype(F32)
    for k in range(1, NZ):
        rz_a[k - 1].wait_recv()
        sum_a = sum_a + r3_a[k].astype(F32)
    for k in range(1, NZ):
        rz_b[k - 1].wait_recv()
        sum_b = sum_b + r3_b[k].astype(F32)
    moe = jnp.concatenate([sum_a[:tok], sum_a[tok:], sum_b[:tok], sum_b[tok:]], axis=-1)
    out_ref[...] = (mixed + moe).astype(BF16)
    for copy in started:
        copy.wait_send()


def local_kernel(
    tokens, attn_gain, w_qkv, q_gain, k_gain, w_out, prefix_keys, prefix_values, segments,
    request_group, prefix_owner, mlp_gain, expert_ids, gate_weights, w_gate, w_up, w_down,
):
    S, T = lax.axis_size("seq"), lax.axis_size("tensor")
    NZ = T // 2
    tok, width = tokens.shape
    cols = w_qkv.shape[2]
    tok_seq = tok * T
    slots = prefix_keys.shape[1]
    units = w_gate.shape[2]
    vm, dma = pltpu.VMEM, pltpu.SemaphoreType.DMA
    quarter = width // 4
    blk = (2 * tok, quarter)
    grid = vm((2, 2, 2, NZ) + blk, BF16)
    pair = lambda *lead: [vm(lead + blk, BF16)] * 2
    scratch = [
        vm((3, width, cols), BF16), vm((cols, width), BF16),
        vm((slots, cols), BF16), vm((slots, cols), BF16),
        vm((width, units), BF16), vm((width, units), BF16), vm((units, width), BF16),
        vm((T, 2 * tok, width // 2), BF16), vm((T, 8, 2 * tok_seq), F32),
        vm((S, 8, 2 * tok_seq), F32), vm((S, 2 * tok_seq, cols), BF16),
        *[vm((S, tok_seq, cols), BF16)] * 3,
        vm((T, 2 * tok, width // 2), BF16), vm((T, 2 * tok, width // 2), BF16),
        grid, grid, vm((2, 2, 2, NZ, tok, 128), F32),
        grid, grid,
        *pair(2, 2, NZ), *pair(2, 2, NZ), *pair(2, NZ),
        *pair(2, NZ), *pair(NZ), *pair(NZ), *pair(NZ),
        dma((7,)),
        *[dma((T,))] * 4, *[dma((S,))] * 8, *[dma((T,))] * 2,
        *[dma((8,))] * 2, *[dma((NZ + 8,))] * 8,
    ]
    in_vmem = pl.BlockSpec(memory_space=pltpu.VMEM)
    in_smem = pl.BlockSpec(memory_space=pltpu.SMEM)
    in_any = pl.BlockSpec(memory_space=pl.ANY)
    results = pl.pallas_call(
        functools.partial(layer_kernel, (S, T, NZ, EXP_DEV)),
        out_shape=(
            jax.ShapeDtypeStruct((tok, width), BF16),
            jax.ShapeDtypeStruct((tok_seq, cols), BF16),
            jax.ShapeDtypeStruct((tok_seq, cols), BF16),
        ),
        in_specs=[in_vmem] * 6 + [in_smem] * 2 + [in_vmem] * 2 + [in_any] * 7,
        out_specs=(in_vmem,) * 3,
        scratch_shapes=scratch,
        compiler_params=pltpu.CompilerParams(
            collective_id=0, has_side_effects=True, vmem_limit_bytes=56 * 2**20
        ),
    )(
        tokens, attn_gain, q_gain, k_gain, mlp_gain,
        segments[None], request_group, prefix_owner, expert_ids, gate_weights,
        jnp.transpose(w_qkv, (1, 0, 2)), w_out, prefix_keys, prefix_values, w_gate, w_up, w_down,
    )
    return pl.pallas_call(
        hand_on,
        out_shape=tuple(jax.ShapeDtypeStruct(r.shape, r.dtype) for r in results),
        in_specs=[in_vmem] * 3,
        out_specs=(in_vmem,) * 3,
    )(*results)


def hand_on(*refs):
    for source, target in zip(refs[:3], refs[3:]):
        target[...] = source[...]


def whole_heads(*arrays):
    seq_size, tensor_size = lax.axis_size("seq"), lax.axis_size("tensor")
    if arrays[2].shape[2] % HD == 0 and seq_size == 4 and tensor_size == 8:
        return local_kernel(*arrays)
    return local(*arrays)


def solution(mesh):
    return jax.shard_map(
        whole_heads,
        mesh=mesh,
        in_specs=(
            P(("seq", "tensor"), None),
            P(),
            P(None, None, "tensor"),
            P("tensor"),
            P("tensor"),
            P("tensor", None),
            P("seq", None, "tensor"),
            P("seq", None, "tensor"),
            P(),
            P(),
            P(),
            P(),
            P(("seq", "tensor"), None),
            P(("seq", "tensor"), None),
            P(("tensor", "seq"), None, None),
            P(("tensor", "seq"), None, None),
            P(("tensor", "seq"), None, None),
        ),
        out_specs=(P(("seq", "tensor"), None), P("seq", "tensor"), P("seq", "tensor")),
        check_vma=False,
    )
```
